256 devices in a mesh: ctx: 64 (over z, y, x_lo), tp: 4 (over x_hi, core).
Axes of the slice: x: 4 (x_hi: 2, x_lo: 2; x = x_hi * 2 + x_lo), y: 4, z: 8, core: 2. Of those that a mesh axis runs over, the one named last changes fastest.
Arguments:
- queries: bfloat16 [256, 128, 128], P('ctx', 'tp'), may hold values from -60 to 60
- cached_keys: bfloat16 [131072, 8, 128], P('ctx', 'tp'), may hold values from -6 to 6
- cached_values: bfloat16 [131072, 8, 128], P('ctx', 'tp'), may hold values from -6 to 6
- cached_pos: int32 [131072], P('ctx'), may hold values from -1 to 131071, as said below
- new_keys: bfloat16 [256, 8, 128], P('ctx', 'tp'), may hold values from -9 to 9
- new_values: bfloat16 [256, 8, 128], P('ctx', 'tp'), may hold values from -6 to 6
- new_pos: int32 [256], replicated, may hold values from 131072 to 131327, as said below
- out_weight: bfloat16 [16384, 16384], P('tp', 'ctx'), may hold values from -0.046875 to 0.046875
Outputs:
- context: bfloat16 [256, 16384], P('ctx', 'tp')
- projected: bfloat16 [256, 16384], P('tp', 'ctx')
The draws below stay inside these ranges and needn't reach their ends.
Inputs may be any that keep to these rules, and one draw needn't show every extreme that they name: `cached_pos`: each index of ctx holds 2048 slots; the filled ones come first in its block, at least a quarter of them; some block is full; filled slots carry distinct positions below 131072. `new_pos`: distinct positions following the cache.
All inputs are finite; a program needn't handle non-finite values.
Results may differ from the reference program's by a relative error of at most 0.015.
Values may be sent and summed in bfloat16 or wider, within the bound.
No kernel may reach another device: no remote copies, remote signals or barrier semaphores. Data moves between devices by JAX's collectives and lax.ppermute only.
A program may use at most 128 MiB of HBM per device.

```python
import math
import jax
import jax.numpy as jnp
from jax import lax

D = 16384
HQ = 128
KVH = 8
DH = 128
CACHE_DEV = 2048
GROUP = 16
CACHE = 131072
NEW = 256


def shared_keys(key):
    return jnp.clip(jax.random.normal(key, (CACHE, KVH, DH), jnp.float32), -6.0, 6.0)


def draw_cached_keys(key, part):
    base = shared_keys(key)
    return base.astype(jnp.bfloat16)


def draw_queries(key, part):
    key = jax.random.fold_in(key, 2)
    result = jnp.clip(3.0 * jax.random.normal(key, (NEW, HQ, DH), jnp.float32), -24.0, 24.0)
    return result.astype(jnp.bfloat16)


def draw_cached_pos(key, part):
    key = jax.random.fold_in(key, 3)
    key_a, key_b, key_c = jax.random.split(key, 3)
    nblk = CACHE // CACHE_DEV
    shifts = jax.random.randint(key_a, (nblk,), 0, 3)
    full_block = jax.random.randint(key_b, (), 0, nblk)
    counts = jnp.right_shift(jnp.full((nblk,), CACHE_DEV, jnp.int32), shifts.astype(jnp.int32))
    counts = jnp.where(jnp.arange(nblk) == full_block, CACHE_DEV, counts)
    slots = jnp.arange(CACHE)
    filled = slots % CACHE_DEV < counts[slots // CACHE_DEV]
    order = jax.random.permutation(key_c, CACHE).astype(jnp.int32)
    target = (full_block * CACHE_DEV).astype(jnp.int32)
    holder = jnp.argmax(order == CACHE - 1).astype(jnp.int32)
    displaced = order[target]
    order = order.at[holder].set(displaced)
    order = order.at[target].set(CACHE - 1)
    return jnp.where(filled, order, -1).astype(jnp.int32)


def draw_new_pos(key, part):
    key = jax.random.fold_in(key, 4)
    return (CACHE + jax.random.permutation(key, NEW)).astype(jnp.int32)


def level_of(own_key, shape, cuts, least, high):
    gain, own = 1.0, jax.random.fold_in(own_key, 6)
    for dim, parts in cuts:
        steps = jnp.exp(jax.random.uniform(jax.random.fold_in(own, dim), (parts,), jnp.float32, least / len(cuts), high / len(cuts)))
        gain = gain * jnp.repeat(steps, shape[dim] // parts).reshape([-1 if axis == dim else 1 for axis in range(len(shape))])
    return gain


def gaussian(stream_key, shape, width, limit, pieces=(), dtype=jnp.bfloat16):
    values = jax.random.normal(stream_key, shape, jnp.float32) * width
    if len(pieces) > 0:
        values = level_of(stream_key, shape, pieces, -0.22, 0.18) * values
    return jnp.clip(values, min=-limit, max=limit).astype(dtype)


def setup_inputs(seed: int = 0) -> dict:
    streams_of = jax.random.split(jax.random.key(seed), 9)
    queries = draw_queries(jax.random.fold_in(streams_of[8], 71), 0)
    cached_keys = draw_cached_keys(jax.random.fold_in(streams_of[8], 71), 0)
    cached_values = gaussian(streams_of[2], (CACHE, KVH, DH), 1.0, 6.0, ((0, 64), (1, 4)))
    cached_pos = draw_cached_pos(jax.random.fold_in(streams_of[8], 71), 0)
    new_keys = gaussian(streams_of[4], (NEW, KVH, DH), 1.6, 9.0, ((0, 64), (1, 4)))
    new_values = gaussian(streams_of[5], (NEW, KVH, DH), 1.0, 6.0, ((0, 64), (1, 4)))
    new_pos = draw_new_pos(jax.random.fold_in(streams_of[8], 71), 0)
    out_weight = gaussian(streams_of[7], (HQ * DH, D), (HQ * DH) ** -0.5, 0.046875, ((0, 4), (1, 64)))
    return {"queries": queries, "cached_keys": cached_keys, "cached_values": cached_values, "cached_pos": cached_pos, "new_keys": new_keys, "new_values": new_values, "new_pos": new_pos, "out_weight": out_weight}


masked_score = -1e+30

def tile(q4, keys, values, qpos, kpos, scale):
    s = jnp.einsum('rhgd,khd->rhgk', q4.astype(jnp.float32), keys.astype(jnp.float32), precision=lax.Precision.HIGHEST) * scale
    allow = ((kpos[None, :] >= 0) & (kpos[None, :] <= qpos[:, None]))[:, None, None, :]
    s = jnp.where(allow, s, masked_score)
    top = lax.optimization_barrier(jnp.max(s, axis=-1))
    weights = jnp.where(allow, jnp.exp(s - top[..., None]), 0.0)
    total = lax.optimization_barrier(jnp.sum(weights, axis=-1))
    rounded = lax.optimization_barrier(weights.astype(jnp.bfloat16)).astype(jnp.float32)
    numer = jnp.einsum('rhgk,khd->rhgd', rounded, values.astype(jnp.float32), precision=lax.Precision.HIGHEST)
    return (numer, top, total)

def combine_parts(first, second):
    top = jnp.maximum(first[1], second[1])
    factor_a = jnp.exp(first[1] - top)
    factor_b = jnp.exp(second[1] - top)
    numer = first[0] * factor_a[..., None] + second[0] * factor_b[..., None]
    return (numer, top, first[2] * factor_a + second[2] * factor_b)

def reference(queries, cached_keys, cached_values, cached_pos, new_keys, new_values, new_pos, out_weight):
    scale = 1.0 / math.sqrt(DH)
    q4 = queries.reshape(NEW, KVH, GROUP, DH)
    block = math.gcd(CACHE_DEV, 512)
    nblk = CACHE // block
    key_blocks = cached_keys.reshape(nblk, block, KVH, DH)
    value_blocks = cached_values.reshape(nblk, block, KVH, DH)
    pos_blocks = cached_pos.reshape(nblk, block)
    start = (jnp.zeros((NEW, KVH, GROUP, DH), jnp.float32), jnp.full((NEW, KVH, GROUP), masked_score, jnp.float32), jnp.zeros((NEW, KVH, GROUP), jnp.float32))

    def step(carry, blk):
        return (combine_parts(carry, tile(q4, blk[0], blk[1], new_pos, blk[2], scale)), None)
    carry, _ = lax.scan(step, start, (key_blocks, value_blocks, pos_blocks))
    carry = combine_parts(carry, tile(q4, new_keys, new_values, new_pos, new_pos, scale))
    context = (carry[0] / carry[2][..., None]).astype(jnp.bfloat16).reshape(NEW, HQ * DH)
    projected = jnp.dot(context, out_weight, preferred_element_type=jnp.float32).astype(jnp.bfloat16)
    return (context, projected)
```

```python
import functools
import math

import jax
import jax.numpy as jnp
import numpy as np
from jax import lax
from jax.experimental import pallas as pl
from jax.experimental.pallas import tpu as pltpu
from jax.sharding import Mesh, PartitionSpec as P

bf16 = jnp.bfloat16
f32 = jnp.float32
masked_score = -1e30
VMEM = pl.BlockSpec(memory_space=pltpu.VMEM)
SMEM = pl.BlockSpec(memory_space=pltpu.SMEM)


def eye_mask():
    shape = (128, 128)
    return lax.broadcasted_iota(jnp.int32, shape, 0) == lax.broadcasted_iota(jnp.int32, shape, 1)


def split3(x):
    hi = x.astype(bf16).astype(f32)
    mid = (x - hi).astype(bf16).astype(f32)
    return hi, mid, x - hi - mid


def pack_stats(lse):
    hi, mid, lo = split3(lse)
    return jnp.concatenate([hi, mid, lo, jnp.zeros((8, 128), f32)], axis=0).astype(bf16)


def unpack_stats(packed):
    x = packed.astype(f32)
    return x[0:8] + x[8:16] + x[16:24]


def attention_kernel(
    tokens, chunk, scale2, plane_ref, q_ref, kt_ref, vx_ref, kn_ref, vn_ref, tok_ref, kpos_ref, o_ref, st_ref
):
    rows = chunk * 16
    eye = eye_mask()
    base = plane_ref[0] * tokens

    def scores(h, t0):
        q = q_ref[t0 : t0 + chunk, 16 * h : 16 * h + 16, :].reshape(rows, 128)
        s = jnp.dot(q, kt_ref[h], preferred_element_type=f32)
        sn = jnp.dot(q, kn_ref[h], preferred_element_type=f32)
        allow = kpos_ref[...].reshape(1, 1, 128) <= tok_ref[pl.ds(base + t0, chunk)]
        allow = jnp.broadcast_to(allow, (chunk, 16, 128))
        sn = jnp.where(allow, sn.reshape(chunk, 16, 128), masked_score).reshape(rows, 128)
        return s, sn

    def finish(h, t0, s, sn):
        top = jnp.maximum(jnp.max(s, axis=1, keepdims=True), jnp.max(sn, axis=1, keepdims=True))
        top = top * scale2
        p = jnp.exp2(s * scale2 - top).astype(bf16)
        pn = jnp.exp2(sn * scale2 - top).astype(bf16)
        acc = jnp.dot(p, vx_ref[h], preferred_element_type=f32)
        acc = acc + jnp.dot(pn, vn_ref[h], preferred_element_type=f32)
        total = acc[:, 128:]
        out = (acc[:, :128] / total).astype(bf16)
        o_ref[t0 : t0 + chunk, 16 * h : 16 * h + 16, :] = out.reshape(chunk, 16, 128)
        lse = top + jnp.log2(total)
        for i in range(rows // 128):
            row = jnp.sum(jnp.where(eye, lse[128 * i : 128 * i + 128], 0.0), axis=0, keepdims=True)
            st_ref[pl.ds((h * tokens + t0) // 8 + i, 1), :] = row

    prev = None
    for t0 in range(0, tokens, chunk):
        for h in range(2):
            s, sn = scores(h, t0)
            if prev is not None:
                finish(*prev)
            prev = (h, t0, s, sn)
    finish(*prev)
    o_ref[tokens] = pack_stats(st_ref[...])


def attention(plane, q, kt, vx, kn, vn, tok, kpos):
    tokens = q.shape[0]
    scale2 = math.log2(math.e) / math.sqrt(128)
    return pl.pallas_call(
        functools.partial(attention_kernel, tokens, 16, scale2),
        out_shape=jax.ShapeDtypeStruct((tokens + 1, 32, 128), bf16),
        in_specs=[SMEM] + [VMEM] * 7,
        out_specs=VMEM,
        scratch_shapes=[pltpu.VMEM((8, 128), f32)],
        compiler_params=pltpu.CompilerParams(vmem_limit_bytes=40 * 1024 * 1024),
        cost_estimate=pl.CostEstimate(flops=3_000_000_000, bytes_accessed=4_000_000, transcendentals=0),
        name="attention_block",
    )(plane, q, kt, vx, kn, vn, tok, kpos)


def weights_of(lses):
    top = functools.reduce(jnp.maximum, lses)
    parts = [jnp.exp2(x - top) for x in lses]
    total = functools.reduce(jnp.add, parts)
    return [x / total for x in parts], top + jnp.log2(total)


def mix(eye, weights, blocks):
    acc = jnp.zeros((128, 128), f32)
    for w, b in zip(weights, blocks):
        d = jnp.where(eye, jnp.broadcast_to(w, (128, 128)), 0.0)
        hi = d.astype(bf16)
        lo = (d - hi.astype(f32)).astype(bf16)
        acc = acc + jnp.dot(hi, b, preferred_element_type=f32)
        acc = acc + jnp.dot(lo, b, preferred_element_type=f32)
    return acc.astype(bf16)


def plane_kernel(n, *refs):
    msgs, outs, st_ref = refs[:n], refs[n : n + 4], refs[n + 4]
    eye = eye_mask()
    weights, lse = weights_of([unpack_stats(m[32]) for m in msgs])
    st_ref[...] = jnp.zeros((8, 128), f32)
    for quarter in range(4):
        for h in range(2):
            i = 4 * h + quarter
            t = slice(8 * quarter, 8 * quarter + 8)
            g = slice(16 * h, 16 * h + 16)
            blocks = [m[t, g, :].reshape(128, 128) for m in msgs]
            out = mix(eye, [w[i : i + 1] for w in weights], blocks)
            outs[quarter][0:8, g, :] = out.reshape(8, 16, 128)
            st_ref[h : h + 1, :] = lse[i : i + 1]
        outs[quarter][8] = pack_stats(st_ref[...])


def plane_combine(msgs):
    n = len(msgs)
    return pl.pallas_call(
        functools.partial(plane_kernel, n),
        out_shape=tuple(jax.ShapeDtypeStruct((9, 32, 128), bf16) for _ in range(4)),
        in_specs=[VMEM] * n,
        out_specs=tuple(VMEM for _ in range(4)),
        scratch_shapes=[pltpu.VMEM((8, 128), f32)],
        compiler_params=pltpu.CompilerParams(vmem_limit_bytes=24 * 1024 * 1024),
        cost_estimate=pl.CostEstimate(flops=500_000_000, bytes_accessed=3_000_000, transcendentals=0),
        name="plane_combine",
    )(*msgs)


def row_kernel(n, *refs):
    msgs, out = refs[:n], refs[n]
    eye = eye_mask()
    weights, lse = weights_of([unpack_stats(m[8]) for m in msgs])
    for h in range(2):
        g = slice(16 * h, 16 * h + 16)
        blocks = [m[0:8, g, :].reshape(128, 128) for m in msgs]
        out[0:8, g, :] = mix(eye, [w[h : h + 1] for w in weights], blocks).reshape(8, 16, 128)
    out[8] = pack_stats(lse)


def row_combine(msgs):
    n = len(msgs)
    return pl.pallas_call(
        functools.partial(row_kernel, n),
        out_shape=jax.ShapeDtypeStruct((9, 32, 128), bf16),
        in_specs=[VMEM] * n,
        out_specs=VMEM,
        compiler_params=pltpu.CompilerParams(vmem_limit_bytes=8 * 1024 * 1024),
        name="row_combine",
    )(*msgs)


def pair_kernel(mine, other, out):
    eye = eye_mask()
    theirs = unpack_stats(other[8])
    theirs = jnp.concatenate([theirs[:, 64:], theirs[:, :64]], axis=1)
    weights, _ = weights_of([unpack_stats(mine[8]), theirs])
    for h in range(2):
        g = slice(16 * h, 16 * h + 16)
        a = mine[0:8, g, :].reshape(128, 128)
        b = jnp.concatenate([other[4:8, g, :], other[0:4, g, :]], axis=0).reshape(128, 128)
        out[:, g, :] = mix(eye, [w[h : h + 1] for w in weights], [a, b]).reshape(8, 16, 128)


def pair_combine(mine, other):
    return pl.pallas_call(
        pair_kernel,
        out_shape=jax.ShapeDtypeStruct((8, 32, 128), bf16),
        in_specs=[VMEM] * 2,
        out_specs=VMEM,
        compiler_params=pltpu.CompilerParams(vmem_limit_bytes=8 * 1024 * 1024),
        name="pair_combine",
    )(mine, other)


def shift(x, axis, k, size):
    return lax.ppermute(x, axis, [(i, (i + k) % size) for i in range(size)])


def per_device(queries, cached_keys, cached_values, cached_pos, new_keys, new_values, new_pos, out_weight):
    z, y, xl = lax.axis_index("z"), lax.axis_index("y"), lax.axis_index("xl")

    pair = jnp.concatenate([queries, shift(queries, "xl", 1, 2)], axis=0)
    block = jnp.concatenate([pair] + [shift(pair, "y", -k, 4) for k in (1, 2, 3)], axis=0)

    valid = (cached_pos >= 0)[:, None, None]
    kt = jnp.transpose(jnp.where(valid, cached_keys, cached_keys[0:1]), (1, 2, 0))
    v = jnp.transpose(jnp.where(valid, cached_values, 0), (1, 0, 2))
    count = jnp.broadcast_to((cached_pos >= 0).astype(bf16)[None, :, None], (2, 2048, 128))
    vx = jnp.concatenate([v, count], axis=2)
    kn = jnp.pad(jnp.transpose(new_keys, (1, 2, 0)), ((0, 0), (0, 0), (0, 124)))
    vn = jnp.concatenate([jnp.transpose(new_values, (1, 0, 2)), jnp.ones((2, 4, 128), bf16)], axis=2)
    vn = jnp.pad(vn, ((0, 0), (0, 124), (0, 0)))

    home = (z * 4 + y) * 2 + xl
    own_pos = lax.dynamic_slice_in_dim(new_pos, home * 4, 4)
    kpos = jnp.concatenate([own_pos, jnp.full((124,), 2**30, jnp.int32)])[None]
    rel = jnp.arange(256)
    order = (rel // 32) * 32 + ((rel // 8 + y) % 4) * 8 + ((rel // 4 + xl) % 2) * 4 + rel % 4
    seen = (order[:, None] == rel[None, :]).astype(jnp.int32)
    tok = jnp.sum(seen * new_pos[None, :], axis=1)
    tok = jnp.broadcast_to(tok[:, None, None], (256, 1, 128))

    def attend(q, k):
        plane = ((z + k) % 8).astype(jnp.int32).reshape(1)
        return attention(plane, q, kt, vx, kn, vn, tok, kpos)

    msgs = [attend(block, 0)]
    up, down = block, block
    for s in (1, 2, 3):
        up, down = shift(up, "z", 1, 8), shift(down, "z", -1, 8)
        msgs.append(shift(attend(up, -s), "z", -s, 8))
        msgs.append(shift(attend(down, s), "z", s, 8))
    up = shift(up, "z", 1, 8)
    msgs.append(shift(attend(up, 4), "z", 4, 8))

    quarters = plane_combine(msgs)
    row = row_combine([quarters[0]] + [shift(quarters[k], "y", k, 4) for k in (1, 2, 3)])
    final = pair_combine(row, shift(row, "xl", 1, 2)).reshape(8, 4096)
    context = final[0:4]

    plane = jnp.concatenate([final] + [shift(final, "y", -k, 4) for k in (1, 2, 3)], axis=0)
    ahead, behind = [], []
    up, down = plane, plane
    for s in (1, 2, 3):
        up, down = shift(up, "z", 1, 8), shift(down, "z", -1, 8)
        ahead.append(down)
        behind.append(up)
    far = shift(up, "z", 1, 8)
    near = jnp.concatenate([plane] + ahead + [far] + behind[::-1], axis=0)
    terms = jnp.dot(near, out_weight, preferred_element_type=f32).astype(bf16)

    pick = ((order // 32 + z) % 8) * 32 + order % 32
    place = (pick[None, :] == rel[:, None]).astype(bf16)
    terms = jnp.dot(place, terms, preferred_element_type=f32).astype(bf16)
    parts = lax.all_to_all(terms.reshape(4, 64, 256), ("xh", "core"), 0, 0, tiled=True)
    projected = jnp.sum(parts.astype(f32), axis=0).astype(bf16)
    return (context, projected)


def solution(mesh):
    fine = Mesh(mesh.devices.reshape(8, 4, 2, 2, 2), ("z", "y", "xl", "xh", "core"))
    ctx, tp = ("z", "y", "xl"), ("xh", "core")
    in_specs = (
        P(ctx, tp, None),
        P(ctx, tp, None),
        P(ctx, tp, None),
        P(ctx),
        P(ctx, tp, None),
        P(ctx, tp, None),
        P(),
        P(tp, ctx),
    )
    out_specs = (P(ctx, tp), P(tp, ctx))
    return jax.shard_map(per_device, mesh=fine, in_specs=in_specs, out_specs=out_specs, check_vma=False)
```

```python
import functools
import math

import jax
import jax.numpy as jnp
from jax import lax
from jax.experimental import pallas as pl
from jax.experimental.pallas import tpu as pltpu
from jax.sharding import Mesh, PartitionSpec as P

bf16 = jnp.bfloat16
f32 = jnp.float32
masked_score = -1e30
VMEM = pl.BlockSpec(memory_space=pltpu.VMEM)
SMEM = pl.BlockSpec(memory_space=pltpu.SMEM)
ANY = pl.BlockSpec(memory_space=pl.ANY)
MIB = 1024 * 1024

offsets = (0, -1, 1, -2, 2, -3, 3, 4)


def iota(shape, dim):
    return lax.broadcasted_iota(jnp.int32, shape, dim)


def split3(x):
    hi = x.astype(bf16).astype(f32)
    mid = (x - hi).astype(bf16).astype(f32)
    return hi, mid, x - hi - mid


def attention_kernel(
    scale2, fresh, idx_ref, q_ref, kt_ref, vx_ref, kn_ref, vn_ref, tok_ref, kpos_ref, *refs
):
    outs, st_ref, pack_ref = refs[fresh : fresh + 4], refs[fresh + 4], refs[fresh + 5]
    plane, y = idx_ref[0], idx_ref[1]
    row, lane = iota((64, 128), 0), iota((64, 128), 1)
    spots = [lane == (row // 16) * 32 + 16 * h + row % 16 for h in range(2)]

    def scores(c, h):
        starts = [((y + 2 * c + k) % 4) * 8 for k in range(2)]
        q = jnp.concatenate([q_ref[pl.ds(s, 8), 16 * h : 16 * h + 16, :] for s in starts], axis=0)
        q = q.reshape(256, 128)
        s = jnp.dot(q, kt_ref[h], preferred_element_type=f32)
        sn = jnp.dot(q, kn_ref[h], preferred_element_type=f32)
        tok = jnp.concatenate([tok_ref[pl.ds(plane * 32 + s, 8)] for s in starts], axis=0)
        allow = jnp.broadcast_to(kpos_ref[...].reshape(1, 1, 128) <= tok, (16, 16, 128))
        sn = jnp.where(allow, sn.reshape(16, 16, 128), masked_score).reshape(256, 128)
        return s, sn

    def finish(c, h, s, sn):
        top = jnp.maximum(jnp.max(s, axis=1, keepdims=True), jnp.max(sn, axis=1, keepdims=True))
        top = top * scale2
        p = jnp.exp2(s * scale2 - top).astype(bf16)
        pn = jnp.exp2(sn * scale2 - top).astype(bf16)
        acc = jnp.dot(p, vx_ref[h], preferred_element_type=f32)
        acc = acc + jnp.dot(pn, vn_ref[h], preferred_element_type=f32)
        total = acc[:, 128:]
        out = (acc[:, :128] / total).astype(bf16)
        for k in range(2):
            for t in range(8):
                at = t * 32 + 16 * h
                outs[2 * c + k][0, at : at + 16, :] = out[(k * 8 + t) * 16 : (k * 8 + t) * 16 + 16]
        lse = top + jnp.log2(total)
        for j in range(4):
            part = jnp.sum(jnp.where(spots[h], lse[64 * j : 64 * j + 64], 0.0), axis=0, keepdims=True)
            i = 4 * c + j
            if h == 1:
                part = part + st_ref[i : i + 1, :]
            st_ref[i : i + 1, :] = part

    prev = None
    for c in range(2):
        for h in range(2):
            s, sn = scores(c, h)
            if prev is not None:
                finish(*prev)
            prev = (c, h, s, sn)
    finish(*prev)
    pack_ref[...] = jnp.zeros((16, 128), f32)
    parts = split3(st_ref[...])
    for k in range(4):
        for n, x in enumerate(parts):
            pack_ref[2 * n : 2 * n + 2, :] = x[2 * k : 2 * k + 2]
        outs[k][0, 256:272, :] = pack_ref[...].astype(bf16)


def attention(slot, idx, q, fixed, prior):
    half = slot % 4
    shapes = [8, 8, 4, 8]
    places = [slot, slot, half, slot]
    prior = [p for p in prior if p is not None]
    aliases, at = {}, 0
    if len(prior) == 4:
        aliases = {8 + i: i for i in range(4)}
    elif len(prior) == 3:
        aliases = {8: 0, 9: 1, 10: 3}
    return pl.pallas_call(
        functools.partial(attention_kernel, math.log2(math.e) / math.sqrt(128), len(prior)),
        grid=(1,),
        out_shape=tuple(jax.ShapeDtypeStruct((n, 272, 128), bf16) for n in shapes),
        in_specs=[SMEM] + [VMEM] * 7 + [ANY] * len(prior),
        out_specs=tuple(
            pl.BlockSpec((1, 272, 128), functools.partial(lambda p, i: (p, 0, 0), p)) for p in places
        ),
        scratch_shapes=[pltpu.VMEM((8, 128), f32), pltpu.VMEM((16, 128), f32)],
        input_output_aliases=aliases,
        compiler_params=pltpu.CompilerParams(vmem_limit_bytes=40 * MIB),
        cost_estimate=pl.CostEstimate(flops=3_000_000_000, bytes_accessed=4_000_000, transcendentals=0),
        name="attention_block",
    )(idx, q, *fixed, *prior)


def mix(eye, weights, blocks):
    acc = jnp.zeros((128, 128), f32)
    for w, b in zip(weights, blocks):
        d = jnp.where(eye, jnp.broadcast_to(w, (128, 128)), 0.0)
        hi = d.astype(bf16)
        lo = (d - hi.astype(f32)).astype(bf16)
        acc = acc + jnp.dot(hi, b, preferred_element_type=f32)
        acc = acc + jnp.dot(lo, b, preferred_element_type=f32)
    return acc.astype(bf16)


def slab_kernel(idx_ref, m0, m1, m2a, m2b, m3, out_ref, st_ref, pack_ref):
    z = idx_ref[0]
    eye = iota((128, 128), 0) == iota((128, 128), 1)
    row = iota((16, 128), 0)

    def sources(slot):
        far = (m2a, slot) if slot < 4 else (m2b, slot - 4)
        return [(m0, slot), (m1, slot), far, (m3, slot)]

    for slot in range(8):
        for n, (m, s) in enumerate(sources(slot)):
            x = m[s, 256:272, :].astype(f32)
            for j in range(2):
                own = (row < 6) & (row % 2 == j)
                lse = jnp.sum(jnp.where(own, x, 0.0), axis=0, keepdims=True)
                st_ref[n, 2 * slot + j : 2 * slot + j + 1, :] = lse
    lses = [st_ref[n] for n in range(4)]
    top = functools.reduce(jnp.maximum, lses)
    weights = [jnp.exp2(x - top) for x in lses]
    total = functools.reduce(jnp.add, weights)
    weights = [x / total for x in weights]
    parts = split3(top + jnp.log2(total))
    pack_ref[...] = jnp.zeros((16, 128), f32)
    for slot in range(8):
        for j in range(2):
            i = 2 * slot + j
            blocks = [m[s, 128 * j : 128 * j + 128, :] for m, s in sources(slot)]
            at = ((z + 8 + offsets[slot]) % 8) * 2 + j
            out_ref[at, 0:128, :] = mix(eye, [w[i : i + 1] for w in weights], blocks)
            for n, x in enumerate(parts):
                pack_ref[n : n + 1, :] = x[i : i + 1]
            out_ref[at, 128:144, :] = pack_ref[...].astype(bf16)


def slab_combine(idx, msgs):
    return pl.pallas_call(
        slab_kernel,
        out_shape=jax.ShapeDtypeStruct((16, 144, 128), bf16),
        in_specs=[SMEM] + [VMEM] * 5,
        out_specs=VMEM,
        scratch_shapes=[pltpu.VMEM((4, 16, 128), f32), pltpu.VMEM((16, 128), f32)],
        compiler_params=pltpu.CompilerParams(vmem_limit_bytes=24 * MIB),
        cost_estimate=pl.CostEstimate(flops=500_000_000, bytes_accessed=3_000_000, transcendentals=0),
        name="slab_combine",
    )(idx, *msgs)


def home_kernel(m_ref, out_ref, st_ref):
    eye = iota((128, 128), 0) == iota((128, 128), 1)
    for n in range(16):
        x = m_ref[n, 128:144, :].astype(f32)
        st_ref[n : n + 1, :] = jnp.sum(jnp.where(iota((16, 128), 0) < 3, x, 0.0), axis=0, keepdims=True)
    lse = st_ref[...]
    weights = jnp.exp2(lse - jnp.max(lse, axis=0, keepdims=True))
    weights = weights / jnp.sum(weights, axis=0, keepdims=True)
    out_ref[...] = mix(eye, [weights[n : n + 1] for n in range(16)], [m_ref[n, 0:128, :] for n in range(16)])


def home_combine(msgs):
    return pl.pallas_call(
        home_kernel,
        out_shape=jax.ShapeDtypeStruct((128, 128), bf16),
        in_specs=[VMEM],
        out_specs=VMEM,
        scratch_shapes=[pltpu.VMEM((16, 128), f32)],
        compiler_params=pltpu.CompilerParams(vmem_limit_bytes=8 * MIB),
        name="home_combine",
    )(msgs)


def shift(x, axis, k, size):
    return lax.ppermute(x, axis, [(i, (i + k) % size) for i in range(size)])


def spread(x, axes, n):
    return lax.all_to_all(jnp.broadcast_to(x[None], (n,) + x.shape), axes, 0, 0)


def per_device(queries, cached_keys, cached_values, cached_pos, new_keys, new_values, new_pos, out_weight):
    z, y, xl = lax.axis_index("z"), lax.axis_index("y"), lax.axis_index("xl")

    block = spread(queries, ("y", "xl"), 8).reshape(32, 32, 128)

    valid = (cached_pos >= 0)[:, None, None]
    kt = jnp.transpose(jnp.where(valid, cached_keys, cached_keys[0:1]), (1, 2, 0))
    v = jnp.transpose(jnp.where(valid, cached_values, 0), (1, 0, 2))
    count = jnp.broadcast_to((cached_pos >= 0).astype(bf16)[None, :, None], (2, 2048, 128))
    vx = jnp.concatenate([v, count], axis=2)
    kn = jnp.pad(jnp.transpose(new_keys, (1, 2, 0)), ((0, 0), (0, 0), (0, 124)))
    vn = jnp.concatenate([jnp.transpose(new_values, (1, 0, 2)), jnp.ones((2, 4, 128), bf16)], axis=2)
    vn = jnp.pad(vn, ((0, 0), (0, 124), (0, 0)))
    home = (z * 4 + y) * 2 + xl
    own_pos = lax.dynamic_slice_in_dim(new_pos, home * 4, 4)
    kpos = jnp.concatenate([own_pos, jnp.full((124,), 2**30, jnp.int32)])[None]
    tok = jnp.broadcast_to(new_pos[:, None, None], (256, 1, 128))
    fixed = (kt, vx, kn, vn, tok, kpos)

    def attend(slot, q, prior):
        idx = jnp.stack([(z + offsets[slot]) % 8, y]).astype(jnp.int32)
        return attention(slot, idx, q, fixed, prior)

    msgs = attend(0, block, [])
    up, down = block, block
    far_a = None
    for s in (1, 2, 3):
        up, down = shift(up, "z", 1, 8), shift(down, "z", -1, 8)
        msgs = attend(2 * s - 1, up, msgs)
        if s == 2:
            far_a = msgs[2]
            msgs = (msgs[0], msgs[1], None, msgs[3])
        msgs = attend(2 * s, down, msgs)
    msgs = attend(7, shift(up, "z", 1, 8), msgs)

    near = (
        msgs[0],
        shift(msgs[1], "y", 1, 4),
        shift(far_a, "y", 2, 4),
        shift(msgs[2], "y", -2, 4),
        shift(msgs[3], "y", -1, 4),
    )
    pieces = slab_combine(jnp.stack([z, y]).astype(jnp.int32), near)
    final = home_combine(lax.all_to_all(pieces, ("z", "xl"), 0, 0, tiled=True))
    context = final.reshape(4, 4096)

    slab = spread(context, ("z", "xl"), 16).reshape(64, 4096)

    def project(x):
        return jnp.dot(x, out_weight, preferred_element_type=f32).astype(bf16)

    ahead, behind = shift(slab, "y", -1, 4), shift(slab, "y", 1, 4)
    far_lo, far_hi = shift(slab[:32], "y", 2, 4), shift(slab[32:], "y", -2, 4)
    terms = [project(slab), project(ahead), project(far_lo), project(far_hi), project(behind)]
    terms = jnp.concatenate(terms, axis=0)

    rel = jnp.arange(256)
    pick = (rel // 8 % 8) * 32 + ((rel // 64 + y) % 4) * 8 + rel % 8
    place = (pick[None, :] == rel[:, None]).astype(bf16)
    terms = jnp.dot(place, terms, preferred_element_type=f32).astype(bf16)
    parts = lax.all_to_all(terms.reshape(4, 64, 256), ("xh", "core"), 0, 0, tiled=True)
    projected = jnp.sum(parts.astype(f32), axis=0).astype(bf16)
    return (context, projected)


def solution(mesh):
    fine = Mesh(mesh.devices.reshape(8, 4, 2, 2, 2), ("z", "y", "xl", "xh", "core"))
    ctx, tp = ("z", "y", "xl"), ("xh", "core")
    in_specs = (
        P(ctx, tp, None),
        P(ctx, tp, None),
        P(ctx, tp, None),
        P(ctx),
        P(ctx, tp, None),
        P(ctx, tp, None),
        P(),
        P(tp, ctx),
    )
    out_specs = (P(ctx, tp), P(tp, ctx))
    return jax.shard_map(per_device, mesh=fine, in_specs=in_specs, out_specs=out_specs, check_vma=False)
```

```python
import functools
import math

import jax
import jax.numpy as jnp
from jax import lax
from jax.experimental import pallas as pl
from jax.experimental.pallas import tpu as pltpu
from jax.sharding import Mesh, PartitionSpec as P

bf16 = jnp.bfloat16
f32 = jnp.float32
masked_score = -1e30
VMEM = pl.BlockSpec(memory_space=pltpu.VMEM)
SMEM = pl.BlockSpec(memory_space=pltpu.SMEM)
ANY = pl.BlockSpec(memory_space=pl.ANY)
MIB = 1024 * 1024

offsets = (0, -1, 1, -2, 2, -3, 3, 4)
first = 5


def iota(shape, dim):
    return lax.broadcasted_iota(jnp.int32, shape, dim)


def split3(x):
    hi = x.astype(bf16).astype(f32)
    mid = (x - hi).astype(bf16).astype(f32)
    return hi, mid, x - hi - mid


def prepare_kernel(pos_ref, k_ref, v_ref, nk_ref, nv_ref, kt_ref, vx_ref, kn_ref, vn_ref):
    filled = jnp.sum((pos_ref[...] >= 0).astype(jnp.int32))
    step = 512

    def body(i, carry):
        rows = pl.ds(pl.multiple_of(i * step, step), step)
        ok = iota((step, 128), 0) + i * step < filled
        for h in range(2):
            at = slice(128 * h, 128 * h + 128)
            k = k_ref[rows, at].astype(f32)
            kt_ref[h, rows, :] = jnp.where(ok, k, k_ref[0:1, at].astype(f32)).astype(bf16)
            vx_ref[h, rows, 0:128] = jnp.where(ok, v_ref[rows, at].astype(f32), 0.0).astype(bf16)
            vx_ref[h, rows, 128:256] = jnp.where(ok, 1.0, 0.0).astype(bf16)
        return carry

    lax.fori_loop(0, 2048 // step, body, 0)
    nk, nv = nk_ref[...].astype(f32), nv_ref[...].astype(f32)
    for h in range(2):
        at = slice(128 * h, 128 * h + 128)
        pad = jnp.zeros((124, 128), f32)
        kn_ref[h] = jnp.concatenate([nk[:, at], pad], axis=0).astype(bf16)
        vn_ref[h, :, 0:128] = jnp.concatenate([nv[:, at], pad], axis=0).astype(bf16)
        vn_ref[h, :, 128:256] = jnp.ones((128, 128), bf16)


def prepare(cached_pos, cached_keys, cached_values, new_keys, new_values):
    return pl.pallas_call(
        prepare_kernel,
        out_shape=(
            jax.ShapeDtypeStruct((2, 2048, 128), bf16),
            jax.ShapeDtypeStruct((2, 2048, 256), bf16),
            jax.ShapeDtypeStruct((2, 128, 128), bf16),
            jax.ShapeDtypeStruct((2, 128, 256), bf16),
        ),
        in_specs=[VMEM] * 5,
        out_specs=(VMEM,) * 4,
        compiler_params=pltpu.CompilerParams(vmem_limit_bytes=24 * MIB),
        cost_estimate=pl.CostEstimate(flops=500_000_000, bytes_accessed=6_000_000, transcendentals=0),
        name="prepare",
    )(
        cached_pos.reshape(16, 128),
        cached_keys.reshape(2048, 256),
        cached_values.reshape(2048, 256),
        new_keys.reshape(4, 256),
        new_values.reshape(4, 256),
    )


def dot_t(a, b):
    return lax.dot_general(a, b, (((1,), (1,)), ((), ())), preferred_element_type=f32)


def attention_kernel(offset, fresh, scale2, idx_ref, npos_ref, q_ref, kt_ref, vx_ref, kn_ref, vn_ref, *refs):
    outs, pack_ref = refs[fresh : fresh + 4], refs[fresh + 4]
    plane, y, home = (idx_ref[0] + 8 + offset) % 8, idx_ref[1], idx_ref[2]
    lane = iota((16, 128), 1)
    kpos = jnp.full((16, 128), 2**30, jnp.int32)
    for j in range(4):
        kpos = jnp.where(lane == j, npos_ref[home * 4 + j], kpos)
    eye = iota((128, 128), 0) == iota((128, 128), 1)
    pack_ref[...] = jnp.zeros(pack_ref.shape, f32)

    def scores(c, h):
        starts = [((y + 2 * c + k) % 4) * 8 for k in range(2)]
        q = jnp.concatenate([q_ref[pl.ds(s, 8), 16 * h : 16 * h + 16, :] for s in starts], axis=0)
        q = q.reshape(256, 128)
        s = dot_t(q, kt_ref[h])
        sn = dot_t(q, kn_ref[h])
        parts = []
        for i in range(16):
            allow = kpos <= npos_ref[plane * 32 + starts[i // 8] + i % 8]
            parts.append(jnp.where(allow, sn[16 * i : 16 * i + 16], masked_score))
        return s, jnp.concatenate(parts, axis=0)

    def finish(c, h, s, sn):
        top = jnp.maximum(jnp.max(s, axis=1, keepdims=True), jnp.max(sn, axis=1, keepdims=True))
        top = top * scale2
        p = jnp.exp2(s * scale2 - top).astype(bf16)
        pn = jnp.exp2(sn * scale2 - top).astype(bf16)
        acc = jnp.dot(p, vx_ref[h], preferred_element_type=f32)
        acc = acc + jnp.dot(pn, vn_ref[h], preferred_element_type=f32)
        total = acc[:, 128:]
        out = (acc[:, :128] / total).astype(bf16)
        lse = top + jnp.log2(total)
        for k in range(2):
            at = slice(128 * k, 128 * k + 128)
            outs[2 * c + k][0, 128 * h : 128 * h + 128, :] = out[at]
            row = jnp.sum(jnp.where(eye, lse[at], 0.0), axis=0, keepdims=True)
            for n, x in enumerate(split3(row)):
                pack_ref[2 * c + k, 2 * n + h : 2 * n + h + 1, :] = x

    prev = None
    for c in range(2):
        for h in range(2):
            s, sn = scores(c, h)
            if prev is not None:
                finish(*prev)
            prev = (c, h, s, sn)
    finish(*prev)
    for k in range(4):
        outs[k][0, 256:272, :] = pack_ref[k].astype(bf16)


def attention(slot, idx, new_pos, q, fixed, prior):
    part, at = (first, slot) if slot < first else (8 - first, slot - first)
    shape = jax.ShapeDtypeStruct((part, 272, 128), bf16)
    return pl.pallas_call(
        functools.partial(
            attention_kernel, offsets[slot], len(prior), math.log2(math.e) / math.sqrt(128)
        ),
        grid=(1,),
        out_shape=(shape,) * 4,
        in_specs=[SMEM] * 2 + [VMEM] * 5 + [ANY] * len(prior),
        out_specs=(pl.BlockSpec((1, 272, 128), lambda i: (at, 0, 0)),) * 4,
        scratch_shapes=[pltpu.VMEM((4, 16, 128), f32)],
        input_output_aliases={7 + i: i for i in range(len(prior))},
        compiler_params=pltpu.CompilerParams(vmem_limit_bytes=40 * MIB),
        cost_estimate=pl.CostEstimate(flops=3_000_000_000, bytes_accessed=4_000_000, transcendentals=0),
        name="attention_block",
    )(idx, new_pos, q, *fixed, *prior)


def mix(eye, weights, blocks):
    acc = jnp.zeros((128, 128), f32)
    for w, b in zip(weights, blocks):
        d = jnp.where(eye, jnp.broadcast_to(w, (128, 128)), 0.0)
        hi = d.astype(bf16)
        lo = (d - hi.astype(f32)).astype(bf16)
        acc = acc + jnp.dot(hi, b, preferred_element_type=f32)
        acc = acc + jnp.dot(lo, b, preferred_element_type=f32)
    return acc.astype(bf16)


def slab_kernel(idx_ref, *refs):
    msgs, out_ref, st_ref, pack_ref = refs[:8], refs[8], refs[9], refs[10]
    z = idx_ref[0]
    eye = iota((128, 128), 0) == iota((128, 128), 1)
    row = iota((16, 128), 0)

    def sources(slot):
        if slot < first:
            return [(m, slot) for m in msgs[:4]]
        return [(m, slot - first) for m in msgs[4:]]

    for slot in range(8):
        for n, (m, s) in enumerate(sources(slot)):
            x = m[s, 256:272, :].astype(f32)
            for h in range(2):
                own = (row < 6) & (row % 2 == h)
                lse = jnp.sum(jnp.where(own, x, 0.0), axis=0, keepdims=True)
                st_ref[n, 2 * slot + h : 2 * slot + h + 1, :] = lse
    lses = [st_ref[n] for n in range(4)]
    top = functools.reduce(jnp.maximum, lses)
    weights = [jnp.exp2(x - top) for x in lses]
    total = functools.reduce(jnp.add, weights)
    weights = [x / total for x in weights]
    parts = split3(top + jnp.log2(total))
    pack_ref[...] = jnp.zeros((2, 16, 128), f32)
    for slot in range(8):
        at = ((z + 8 + offsets[slot]) % 8) * 2
        for h in range(2):
            i = 2 * slot + h
            blocks = [m[s, 128 * h : 128 * h + 128, :] for m, s in sources(slot)]
            mixed = mix(eye, [w[i : i + 1] for w in weights], blocks)
            for j in range(2):
                out_ref[at + j, 64 * h : 64 * h + 64, :] = mixed[64 * j : 64 * j + 64]
        i = 2 * slot
        for n, x in enumerate(parts):
            a, b = x[i : i + 1], x[i + 1 : i + 2]
            pack_ref[0, n : n + 1, :] = jnp.concatenate([a[:, :64], b[:, :64]], axis=1)
            pack_ref[1, n : n + 1, :] = jnp.concatenate([a[:, 64:], b[:, 64:]], axis=1)
        for j in range(2):
            out_ref[at + j, 128:144, :] = pack_ref[j].astype(bf16)


def slab_combine(idx, msgs):
    return pl.pallas_call(
        slab_kernel,
        out_shape=jax.ShapeDtypeStruct((16, 144, 128), bf16),
        in_specs=[SMEM] + [VMEM] * 8,
        out_specs=VMEM,
        scratch_shapes=[pltpu.VMEM((4, 16, 128), f32), pltpu.VMEM((2, 16, 128), f32)],
        compiler_params=pltpu.CompilerParams(vmem_limit_bytes=24 * MIB),
        cost_estimate=pl.CostEstimate(flops=500_000_000, bytes_accessed=3_000_000, transcendentals=0),
        name="slab_combine",
    )(idx, *msgs)


def home_kernel(m_ref, out_ref, st_ref):
    eye = iota((128, 128), 0) == iota((128, 128), 1)
    for n in range(16):
        x = m_ref[n, 128:144, :].astype(f32)
        st_ref[n : n + 1, :] = jnp.sum(jnp.where(iota((16, 128), 0) < 3, x, 0.0), axis=0, keepdims=True)
    lse = st_ref[...]
    weights = jnp.exp2(lse - jnp.max(lse, axis=0, keepdims=True))
    weights = weights / jnp.sum(weights, axis=0, keepdims=True)
    mixed = mix(eye, [weights[n : n + 1] for n in range(16)], [m_ref[n, 0:128, :] for n in range(16)])
    for h in range(2):
        for t in range(4):
            at = 64 * h + 16 * t
            out_ref[t, 16 * h : 16 * h + 16, :] = mixed[at : at + 16]


def home_combine(msgs):
    return pl.pallas_call(
        home_kernel,
        out_shape=jax.ShapeDtypeStruct((4, 32, 128), bf16),
        in_specs=[VMEM],
        out_specs=VMEM,
        scratch_shapes=[pltpu.VMEM((16, 128), f32)],
        compiler_params=pltpu.CompilerParams(vmem_limit_bytes=8 * MIB),
        name="home_combine",
    )(msgs)


def shift(x, axis, k, size):
    return lax.ppermute(x, axis, [(i, (i + k) % size) for i in range(size)])


def spread(x, axes, n):
    return lax.all_to_all(jnp.broadcast_to(x[None], (n,) + x.shape), axes, 0, 0)


def per_device(queries, cached_keys, cached_values, cached_pos, new_keys, new_values, new_pos, out_weight):
    z, y, xl = lax.axis_index("z"), lax.axis_index("y"), lax.axis_index("xl")
    idx = jnp.stack([z, y, (z * 4 + y) * 2 + xl]).astype(jnp.int32)

    block = spread(queries, ("y", "xl"), 8).reshape(32, 32, 128)
    fixed = prepare(cached_pos, cached_keys, cached_values, new_keys, new_values)

    other_weight = shift(out_weight, "xl", 1, 2)

    msgs = attention(0, idx, new_pos, block, fixed, ())
    up, down = block, block
    part = None
    for s in (1, 2, 3):
        up, down = shift(up, "z", 1, 8), shift(down, "z", -1, 8)
        msgs = attention(2 * s - 1, idx, new_pos, up, fixed, msgs)
        msgs = attention(2 * s, idx, new_pos, down, fixed, msgs)
        if s == 2:
            part, msgs = msgs, ()
    up, other_weight = lax.optimization_barrier((shift(up, "z", 1, 8), other_weight))
    msgs = attention(7, idx, new_pos, up, fixed, msgs)

    near = [part[0], shift(part[1], "y", 1, 4), shift(part[2], "y", 2, 4), shift(part[3], "y", -1, 4)]
    near += [msgs[0], shift(msgs[1], "y", 1, 4), shift(msgs[2], "y", -2, 4), shift(msgs[3], "y", -1, 4)]
    pieces = slab_combine(idx, near)

    final = home_combine(lax.all_to_all(pieces, ("z", "xl"), 0, 0, tiled=True))
    context = final.reshape(4, 4096)
    slab = spread(context, ("z",), 8).reshape(32, 4096)

    def project(x):
        return [jnp.dot(x, w, preferred_element_type=f32).astype(bf16) for w in (out_weight, other_weight)]

    blocks = [slab, shift(slab, "y", -1, 4), shift(slab, "y", 2, 4), shift(slab, "y", 1, 4)]
    terms = [jnp.stack(project(x)).reshape(2, 1, 4, 2, 4, 256) for x in blocks]
    terms = jnp.concatenate(terms + terms[:3], axis=1)
    terms = lax.dynamic_slice_in_dim(terms, (4 - y) % 4, 4, axis=1)
    terms = jnp.where(xl == 0, terms, terms[::-1])
    terms = jnp.transpose(terms, (0, 2, 3, 1, 4, 5)).reshape(8, 32, 256)
    parts = lax.all_to_all(terms, ("xl", "xh", "core"), 0, 0, tiled=True)
    projected = jnp.sum(parts.reshape(2, 4, 8, 4, 256).astype(f32), axis=1).astype(bf16)
    projected = jnp.transpose(projected, (1, 0, 2, 3)).reshape(64, 256)
    return (context, projected)


def solution(mesh):
    fine = Mesh(mesh.devices.reshape(8, 4, 2, 2, 2), ("z", "y", "xl", "xh", "core"))
    ctx, tp = ("z", "y", "xl"), ("xh", "core")
    in_specs = (
        P(ctx, tp, None),
        P(ctx, tp, None),
        P(ctx, tp, None),
        P(ctx),
        P(ctx, tp, None),
        P(ctx, tp, None),
        P(),
        P(tp, ctx),
    )
    out_specs = (P(ctx, tp), P(tp, ctx))
    return jax.shard_map(per_device, mesh=fine, in_specs=in_specs, out_specs=out_specs, check_vma=False)
```

```python
import functools
import math

import jax
import jax.numpy as jnp
from jax import lax
from jax.experimental import pallas as pl
from jax.experimental.pallas import tpu as pltpu
from jax.sharding import Mesh, PartitionSpec as P

bf16 = jnp.bfloat16
f32 = jnp.float32
masked_score = -1e30
VMEM = pl.BlockSpec(memory_space=pltpu.VMEM)
SMEM = pl.BlockSpec(memory_space=pltpu.SMEM)
ANY = pl.BlockSpec(memory_space=pl.ANY)
MIB = 1024 * 1024

offsets = (0, -1, 1, -2, 2, -3, 3, 4)
first = 5


def iota(shape, dim):
    return lax.broadcasted_iota(jnp.int32, shape, dim)


def split3(x):
    hi = x.astype(bf16).astype(f32)
    mid = (x - hi).astype(bf16).astype(f32)
    return hi, mid, x - hi - mid


def prepare_kernel(
    npos_ref, pos_ref, k_ref, v_ref, nk_ref, nv_ref, kt_ref, vx_ref, kn_ref, vn_ref, tok_ref, kpos_ref
):
    z, y, xl = lax.axis_index("z"), lax.axis_index("y"), lax.axis_index("xl")
    lane = iota((16, 128), 1)
    kpos = jnp.full((16, 128), 2**30, jnp.int32)
    for j in range(4):
        kpos = jnp.where(lane == j, npos_ref[((z * 4 + y) * 2 + xl) * 4 + j], kpos)
    kpos_ref[...] = kpos
    for slot in range(8):
        for k in range(4):
            at = ((z + 8 + offsets[slot]) % 8) * 32 + ((y + k) % 4) * 8
            for i in range(8):
                tok_ref[4 * slot + k, i : i + 1, :] = jnp.full((1, 128), npos_ref[at + i], jnp.int32)
    filled = jnp.sum((pos_ref[...] >= 0).astype(jnp.int32))
    step = 512

    def body(i, carry):
        rows = pl.ds(pl.multiple_of(i * step, step), step)
        ok = iota((step, 128), 0) + i * step < filled
        for h in range(2):
            at = slice(128 * h, 128 * h + 128)
            k = k_ref[rows, at].astype(f32)
            kt_ref[h, rows, :] = jnp.where(ok, k, k_ref[0:1, at].astype(f32)).astype(bf16)
            vx_ref[h, rows, 0:128] = jnp.where(ok, v_ref[rows, at].astype(f32), 0.0).astype(bf16)
            vx_ref[h, rows, 128:256] = jnp.where(ok, 1.0, 0.0).astype(bf16)
        return carry

    lax.fori_loop(0, 2048 // step, body, 0)
    nk, nv = nk_ref[...].astype(f32), nv_ref[...].astype(f32)
    for h in range(2):
        at = slice(128 * h, 128 * h + 128)
        pad = jnp.zeros((124, 128), f32)
        kn_ref[h] = jnp.concatenate([nk[:, at], pad], axis=0).astype(bf16)
        vn_ref[h, :, 0:128] = jnp.concatenate([nv[:, at], pad], axis=0).astype(bf16)
        vn_ref[h, :, 128:256] = jnp.ones((128, 128), bf16)


def prepare(new_pos, cached_pos, cached_keys, cached_values, new_keys, new_values):
    return pl.pallas_call(
        prepare_kernel,
        out_shape=(
            jax.ShapeDtypeStruct((2, 2048, 128), bf16),
            jax.ShapeDtypeStruct((2, 2048, 256), bf16),
            jax.ShapeDtypeStruct((2, 128, 128), bf16),
            jax.ShapeDtypeStruct((2, 128, 256), bf16),
            jax.ShapeDtypeStruct((32, 8, 128), jnp.int32),
            jax.ShapeDtypeStruct((16, 128), jnp.int32),
        ),
        in_specs=[SMEM] + [VMEM] * 5,
        out_specs=(VMEM,) * 6,
        compiler_params=pltpu.CompilerParams(vmem_limit_bytes=24 * MIB),
        cost_estimate=pl.CostEstimate(flops=500_000_000, bytes_accessed=6_000_000, transcendentals=0),
        name="prepare",
    )(
        new_pos,
        cached_pos.reshape(16, 128),
        cached_keys.reshape(2048, 256),
        cached_values.reshape(2048, 256),
        new_keys.reshape(4, 256),
        new_values.reshape(4, 256),
    )


def dot_t(a, b):
    return lax.dot_general(a, b, (((1,), (1,)), ((), ())), preferred_element_type=f32)


def attention_core(items, fixed_refs, store, scale2):
    kt_ref, vx_ref, kn_ref, vn_ref, tok_ref, kpos_ref = fixed_refs
    y = lax.axis_index("y")
    kpos = kpos_ref[...]

    def scores(chunk, h):
        heads = slice(16 * h, 16 * h + 16)
        q = [ref[pl.ds(((y + k) % 4) * 8, 8), heads, :] for ref, k, _ in chunk]
        q = jnp.concatenate(q, axis=0).reshape(128 * len(chunk), 128)
        s = dot_t(q, kt_ref[h])
        sn = dot_t(q, kn_ref[h])
        parts = []
        for n, (_, _, row) in enumerate(chunk):
            for i in range(8):
                at = 128 * n + 16 * i
                allow = kpos <= tok_ref[row, i : i + 1, :]
                parts.append(jnp.where(allow, sn[at : at + 16], masked_score))
        return s, jnp.concatenate(parts, axis=0)

    def finish(n, h, s, sn):
        top = jnp.maximum(jnp.max(s, axis=1, keepdims=True), jnp.max(sn, axis=1, keepdims=True))
        top = top * scale2
        p = jnp.exp2(s * scale2 - top).astype(bf16)
        pn = jnp.exp2(sn * scale2 - top).astype(bf16)
        acc = jnp.dot(p, vx_ref[h], preferred_element_type=f32)
        acc = acc + jnp.dot(pn, vn_ref[h], preferred_element_type=f32)
        total = acc[:, 128:]
        store(n, h, (acc[:, :128] / total).astype(bf16), top + jnp.log2(total))

    prev = None
    for n, chunk in enumerate(items):
        for h in range(2):
            s, sn = scores(chunk, h)
            if prev is not None:
                finish(*prev)
            prev = (n, h, s, sn)
    finish(*prev)


def stat_row(eye, lse):
    return jnp.sum(jnp.where(eye, lse, 0.0), axis=0, keepdims=True)


def away_kernel(slot, fresh, scale2, q_ref, *refs):
    outs, pack_ref = refs[6 + fresh : 9 + fresh], refs[9 + fresh]
    eye = iota((128, 128), 0) == iota((128, 128), 1)
    pack_ref[...] = jnp.zeros(pack_ref.shape, f32)

    def store(n, h, out, lse):
        for k in range(3):
            at = slice(128 * k, 128 * k + 128)
            outs[k][0, 128 * h : 128 * h + 128, :] = out[at]
            for m, x in enumerate(split3(stat_row(eye, lse[at]))):
                pack_ref[k, 2 * m + h : 2 * m + h + 1, :] = x

    attention_core([[(q_ref, k, 4 * slot + k) for k in (1, 2, 3)]], refs[:6], store, scale2)
    for k in range(3):
        outs[k][0, 256:272, :] = pack_ref[k].astype(bf16)


def stay_kernel(scale2, *refs):
    out_ref, pack_ref = refs[14], refs[15]
    eye = iota((128, 128), 0) == iota((128, 128), 1)
    pack_ref[...] = jnp.zeros(pack_ref.shape, f32)

    def store(n, h, out, lse):
        for k in range(2):
            at = slice(128 * k, 128 * k + 128)
            out_ref[2 * n + k, 128 * h : 128 * h + 128, :] = out[at]
            for m, x in enumerate(split3(stat_row(eye, lse[at]))):
                pack_ref[2 * n + k, 2 * m + h : 2 * m + h + 1, :] = x

    items = [[(refs[2 * n + k], 0, 4 * (2 * n + k)) for k in range(2)] for n in range(4)]
    attention_core(items, refs[8:14], store, scale2)
    for slot in range(8):
        out_ref[slot, 256:272, :] = pack_ref[slot].astype(bf16)


scale2 = math.log2(math.e) / math.sqrt(128)


def attention_away(slot, q, fixed, prior):
    part, at = (first, slot) if slot < first else (8 - first, slot - first)
    shape = jax.ShapeDtypeStruct((part, 272, 128), bf16)
    return pl.pallas_call(
        functools.partial(away_kernel, slot, len(prior), scale2),
        grid=(1,),
        out_shape=(shape,) * 3,
        in_specs=[VMEM] * 7 + [ANY] * len(prior),
        out_specs=(pl.BlockSpec((1, 272, 128), lambda i: (at, 0, 0)),) * 3,
        scratch_shapes=[pltpu.VMEM((3, 16, 128), f32)],
        input_output_aliases={7 + i: i for i in range(len(prior))},
        compiler_params=pltpu.CompilerParams(vmem_limit_bytes=40 * MIB),
        cost_estimate=pl.CostEstimate(flops=2_300_000_000, bytes_accessed=4_000_000, transcendentals=0),
        name="attention_away",
    )(q, *fixed, *prior)


def attention_stay(blocks, fixed):
    return pl.pallas_call(
        functools.partial(stay_kernel, scale2),
        out_shape=jax.ShapeDtypeStruct((8, 272, 128), bf16),
        in_specs=[VMEM] * 14,
        out_specs=VMEM,
        scratch_shapes=[pltpu.VMEM((8, 16, 128), f32)],
        compiler_params=pltpu.CompilerParams(vmem_limit_bytes=40 * MIB),
        cost_estimate=pl.CostEstimate(flops=6_000_000_000, bytes_accessed=4_000_000, transcendentals=0),
        name="attention_stay",
    )(*blocks, *fixed)


def mix(eye, weights, blocks):
    acc = jnp.zeros((128, 128), f32)
    for w, b in zip(weights, blocks):
        d = jnp.where(eye, jnp.broadcast_to(w, (128, 128)), 0.0)
        hi = d.astype(bf16)
        lo = (d - hi.astype(f32)).astype(bf16)
        acc = acc + jnp.dot(hi, b, preferred_element_type=f32)
        acc = acc + jnp.dot(lo, b, preferred_element_type=f32)
    return acc.astype(bf16)


def slab_kernel(*refs):
    msgs, out_ref, st_ref, pack_ref = refs[:7], refs[7], refs[8], refs[9]
    z = lax.axis_index("z")
    eye = iota((128, 128), 0) == iota((128, 128), 1)
    row = iota((16, 128), 0)

    def sources(slot):
        if slot < first:
            return [(msgs[0], slot)] + [(m, slot) for m in msgs[1:4]]
        return [(msgs[0], slot)] + [(m, slot - first) for m in msgs[4:7]]

    for slot in range(8):
        for n, (m, s) in enumerate(sources(slot)):
            x = m[s, 256:272, :].astype(f32)
            for h in range(2):
                own = (row < 6) & (row % 2 == h)
                lse = jnp.sum(jnp.where(own, x, 0.0), axis=0, keepdims=True)
                st_ref[n, 2 * slot + h : 2 * slot + h + 1, :] = lse
    lses = [st_ref[n] for n in range(4)]
    top = functools.reduce(jnp.maximum, lses)
    weights = [jnp.exp2(x - top) for x in lses]
    total = functools.reduce(jnp.add, weights)
    weights = [x / total for x in weights]
    parts = split3(top + jnp.log2(total))
    pack_ref[...] = jnp.zeros((2, 16, 128), f32)
    for slot in range(8):
        at = ((z + 8 + offsets[slot]) % 8) * 2
        for h in range(2):
            i = 2 * slot + h
            blocks = [m[s, 128 * h : 128 * h + 128, :] for m, s in sources(slot)]
            mixed = mix(eye, [w[i : i + 1] for w in weights], blocks)
            for j in range(2):
                out_ref[at + j, 64 * h : 64 * h + 64, :] = mixed[64 * j : 64 * j + 64]
        i = 2 * slot
        for n, x in enumerate(parts):
            a, b = x[i : i + 1], x[i + 1 : i + 2]
            pack_ref[0, n : n + 1, :] = jnp.concatenate([a[:, :64], b[:, :64]], axis=1)
            pack_ref[1, n : n + 1, :] = jnp.concatenate([a[:, 64:], b[:, 64:]], axis=1)
        for j in range(2):
            out_ref[at + j, 128:144, :] = pack_ref[j].astype(bf16)


def slab_combine(msgs):
    return pl.pallas_call(
        slab_kernel,
        out_shape=jax.ShapeDtypeStruct((16, 144, 128), bf16),
        in_specs=[VMEM] * 7,
        out_specs=VMEM,
        scratch_shapes=[pltpu.VMEM((4, 16, 128), f32), pltpu.VMEM((2, 16, 128), f32)],
        compiler_params=pltpu.CompilerParams(vmem_limit_bytes=24 * MIB),
        cost_estimate=pl.CostEstimate(flops=500_000_000, bytes_accessed=3_000_000, transcendentals=0),
        name="slab_combine",
    )(*msgs)


def home_kernel(m_ref, out_ref, st_ref):
    eye = iota((128, 128), 0) == iota((128, 128), 1)
    for n in range(16):
        x = m_ref[n, 128:144, :].astype(f32)
        st_ref[n : n + 1, :] = jnp.sum(jnp.where(iota((16, 128), 0) < 3, x, 0.0), axis=0, keepdims=True)
    lse = st_ref[...]
    weights = jnp.exp2(lse - jnp.max(lse, axis=0, keepdims=True))
    weights = weights / jnp.sum(weights, axis=0, keepdims=True)
    mixed = mix(eye, [weights[n : n + 1] for n in range(16)], [m_ref[n, 0:128, :] for n in range(16)])
    for h in range(2):
        for t in range(4):
            at = 64 * h + 16 * t
            out_ref[t, 16 * h : 16 * h + 16, :] = mixed[at : at + 16]


def home_combine(msgs):
    return pl.pallas_call(
        home_kernel,
        out_shape=jax.ShapeDtypeStruct((4, 32, 128), bf16),
        in_specs=[VMEM],
        out_specs=VMEM,
        scratch_shapes=[pltpu.VMEM((16, 128), f32)],
        compiler_params=pltpu.CompilerParams(vmem_limit_bytes=8 * MIB),
        name="home_combine",
    )(msgs)


def project_kernel(n, *refs):
    x = jnp.concatenate([r[...] for r in refs[:n]], axis=0)
    for c in range(2):
        y = jnp.dot(x, refs[n + c][...], preferred_element_type=f32).astype(bf16)
        for i in range(n):
            refs[n + 2][c, i] = y[32 * i : 32 * i + 32]


def project(blocks, weights):
    n = len(blocks)
    return pl.pallas_call(
        functools.partial(project_kernel, n),
        out_shape=jax.ShapeDtypeStruct((2, n, 32, 256), bf16),
        in_specs=[VMEM] * (n + 2),
        out_specs=VMEM,
        compiler_params=pltpu.CompilerParams(vmem_limit_bytes=24 * MIB),
        cost_estimate=pl.CostEstimate(flops=1_000_000_000, bytes_accessed=5_000_000, transcendentals=0),
        name="project",
    )(*blocks, *weights)


def shift(x, axis, k, size):
    return lax.ppermute(x, axis, [(i, (i + k) % size) for i in range(size)])


def spread(x, axes, n):
    return lax.all_to_all(jnp.broadcast_to(x[None], (n,) + x.shape), axes, 0, 0)


def per_device(queries, cached_keys, cached_values, cached_pos, new_keys, new_values, new_pos, out_weight):
    z, y, xl = lax.axis_index("z"), lax.axis_index("y"), lax.axis_index("xl")

    block = spread(queries, ("y", "xl"), 8).reshape(32, 32, 128)
    fixed = prepare(new_pos, cached_pos, cached_keys, cached_values, new_keys, new_values)
    other_weight = shift(out_weight, "xl", 1, 2)

    msgs = attention_away(0, block, fixed, ())
    up, down = block, block
    blocks = [block]
    part = None
    for s in (1, 2, 3):
        up, down = shift(up, "z", 1, 8), shift(down, "z", -1, 8)
        blocks += [up, down]
        for slot in (2 * s - 1, 2 * s):
            msgs = attention_away(slot, blocks[slot], fixed, msgs)
            if slot == first - 1:
                part, msgs = msgs, ()
    blocks.append(shift(up, "z", 1, 8))
    msgs = attention_away(7, blocks[7], fixed, msgs)
    stay = attention_stay(blocks, fixed)

    away = [shift(m[k - 1], "y", k, 4) for m in (part, msgs) for k in (1, 2, 3)]
    pieces = slab_combine([stay] + away)
    pieces, other_weight = lax.optimization_barrier((pieces, other_weight))

    final = home_combine(lax.all_to_all(pieces, ("z", "xl"), 0, 0, tiled=True))
    context = final.reshape(4, 4096)
    slab = spread(context, ("z",), 8).reshape(32, 4096)

    ahead, behind, far = shift(slab, "y", -1, 4), shift(slab, "y", 1, 4), shift(slab, "y", 2, 4)
    weights = (out_weight, other_weight)
    near = project((slab, ahead, behind), weights)
    terms = [near[:, 0:1], near[:, 1:2], project((far,), weights), near[:, 2:3]]
    terms = [x.reshape(2, 1, 4, 2, 4, 256) for x in terms]
    terms = jnp.concatenate(terms + terms[:3], axis=1)
    terms = lax.dynamic_slice_in_dim(terms, (4 - y) % 4, 4, axis=1)
    terms = jnp.where(xl == 0, terms, terms[::-1])
    terms = jnp.transpose(terms, (0, 2, 3, 1, 4, 5)).reshape(8, 32, 256)
    parts = lax.all_to_all(terms, ("xl", "xh", "core"), 0, 0, tiled=True)
    projected = jnp.sum(parts.reshape(2, 4, 8, 4, 256).astype(f32), axis=1).astype(bf16)
    projected = jnp.transpose(projected, (1, 0, 2, 3)).reshape(64, 256)
    return (context, projected)


def solution(mesh):
    fine = Mesh(mesh.devices.reshape(8, 4, 2, 2, 2), ("z", "y", "xl", "xh", "core"))
    ctx, tp = ("z", "y", "xl"), ("xh", "core")
    in_specs = (
        P(ctx, tp, None),
        P(ctx, tp, None),
        P(ctx, tp, None),
        P(ctx),
        P(ctx, tp, None),
        P(ctx, tp, None),
        P(),
        P(tp, ctx),
    )
    out_specs = (P(ctx, tp), P(tp, ctx))
    return jax.shard_map(per_device, mesh=fine, in_specs=in_specs, out_specs=out_specs, check_vma=False)
```

```python
import functools
import math

import jax
import jax.numpy as jnp
from jax import lax
from jax.experimental import pallas as pl
from jax.experimental.pallas import tpu as pltpu
from jax.sharding import Mesh, PartitionSpec as P

bf16 = jnp.bfloat16
f32 = jnp.float32
masked_score = -1e30
VMEM = pl.BlockSpec(memory_space=pltpu.VMEM)
SMEM = pl.BlockSpec(memory_space=pltpu.SMEM)
ANY = pl.BlockSpec(memory_space=pl.ANY)
MIB = 1024 * 1024

offsets = (0, -1, 1, -2, 2, -3, 3, 4)
first = 5


def iota(shape, dim):
    return lax.broadcasted_iota(jnp.int32, shape, dim)


def split3(x):
    hi = x.astype(bf16).astype(f32)
    mid = (x - hi).astype(bf16).astype(f32)
    return hi, mid, x - hi - mid


def prepare_kernel(
    npos_ref, pos_ref, k_ref, v_ref, nk_ref, nv_ref, kt_ref, vx_ref, kn_ref, vn_ref, tok_ref, kpos_ref
):
    z, y, xl = lax.axis_index("z"), lax.axis_index("y"), lax.axis_index("xl")
    lane = iota((16, 128), 1)
    kpos = jnp.full((16, 128), 2**30, jnp.int32)
    for j in range(4):
        kpos = jnp.where(lane == j, npos_ref[((z * 4 + y) * 2 + xl) * 4 + j], kpos)
    kpos_ref[...] = kpos
    for slot in range(8):
        for k in range(4):
            at = ((z + 8 + offsets[slot]) % 8) * 32 + ((y + k) % 4) * 8
            for i in range(8):
                tok_ref[4 * slot + k, i : i + 1, :] = jnp.full((1, 128), npos_ref[at + i], jnp.int32)
    filled = jnp.sum((pos_ref[...] >= 0).astype(jnp.int32))
    step = 512
    slot0 = k_ref[0:16, :].astype(f32)[0:1]

    def body(i, carry):
        rows = pl.ds(pl.multiple_of(i * step, step), step)
        ok = iota((step, 128), 0) + i * step < filled
        for h in range(2):
            at = slice(128 * h, 128 * h + 128)
            k = k_ref[rows, at].astype(f32)
            kt_ref[h, rows, :] = jnp.where(ok, k, slot0[:, at]).astype(bf16)
            vx_ref[h, rows, 0:128] = jnp.where(ok, v_ref[rows, at].astype(f32), 0.0).astype(bf16)
            vx_ref[h, rows, 128:256] = jnp.where(ok, 1.0, 0.0).astype(bf16)
        return carry

    lax.fori_loop(0, 2048 // step, body, 0)
    nk, nv = nk_ref[...].astype(f32), nv_ref[...].astype(f32)
    for h in range(2):
        at = slice(128 * h, 128 * h + 128)
        pad = jnp.zeros((124, 128), f32)
        kn_ref[h] = jnp.concatenate([nk[:, at], pad], axis=0).astype(bf16)
        vn_ref[h, :, 0:128] = jnp.concatenate([nv[:, at], pad], axis=0).astype(bf16)
        vn_ref[h, :, 128:256] = jnp.ones((128, 128), bf16)


def prepare(new_pos, cached_pos, cached_keys, cached_values, new_keys, new_values):
    return pl.pallas_call(
        prepare_kernel,
        out_shape=(
            jax.ShapeDtypeStruct((2, 2048, 128), bf16),
            jax.ShapeDtypeStruct((2, 2048, 256), bf16),
            jax.ShapeDtypeStruct((2, 128, 128), bf16),
            jax.ShapeDtypeStruct((2, 128, 256), bf16),
            jax.ShapeDtypeStruct((32, 8, 128), jnp.int32),
            jax.ShapeDtypeStruct((16, 128), jnp.int32),
        ),
        in_specs=[SMEM] + [VMEM] * 5,
        out_specs=(VMEM,) * 6,
        compiler_params=pltpu.CompilerParams(vmem_limit_bytes=24 * MIB),
        cost_estimate=pl.CostEstimate(flops=500_000_000, bytes_accessed=6_000_000, transcendentals=0),
        name="prepare",
    )(
        new_pos,
        cached_pos.reshape(16, 128),
        cached_keys.reshape(2048, 256),
        cached_values.reshape(2048, 256),
        new_keys.reshape(4, 256),
        new_values.reshape(4, 256),
    )


def dot_t(a, b):
    return lax.dot_general(a, b, (((1,), (1,)), ((), ())), preferred_element_type=f32)


def attention_core(items, fixed_refs, store, scale2):
    kt_ref, vx_ref, kn_ref, vn_ref, tok_ref, kpos_ref = fixed_refs
    y = lax.axis_index("y")
    kpos = kpos_ref[...]

    def scores(chunk, h):
        heads = slice(16 * h, 16 * h + 16)
        q = [ref[pl.ds(((y + k) % 4) * 8, 8), heads, :] for ref, k, _ in chunk]
        q = jnp.concatenate(q, axis=0).reshape(128 * len(chunk), 128)
        s = dot_t(q, kt_ref[h])
        sn = dot_t(q, kn_ref[h])
        parts = []
        for n, (_, _, row) in enumerate(chunk):
            for i in range(8):
                at = 128 * n + 16 * i
                allow = kpos <= tok_ref[row, i : i + 1, :]
                parts.append(jnp.where(allow, sn[at : at + 16], masked_score))
        return s, jnp.concatenate(parts, axis=0)

    def finish(n, h, s, sn):
        top = jnp.maximum(jnp.max(s, axis=1, keepdims=True), jnp.max(sn, axis=1, keepdims=True))
        top = top * scale2
        p = jnp.exp2(s * scale2 - top).astype(bf16)
        pn = jnp.exp2(sn * scale2 - top).astype(bf16)
        acc = jnp.dot(p, vx_ref[h], preferred_element_type=f32)
        acc = acc + jnp.dot(pn, vn_ref[h], preferred_element_type=f32)
        total = acc[:, 128:]
        store(n, h, (acc[:, :128] / total).astype(bf16), top + jnp.log2(total))

    prev = None
    for n, chunk in enumerate(items):
        for h in range(2):
            s, sn = scores(chunk, h)
            if prev is not None:
                finish(*prev)
            prev = (n, h, s, sn)
    finish(*prev)


def stat_row(eye, lse):
    return jnp.sum(jnp.where(eye, lse, 0.0), axis=0, keepdims=True)


def away_kernel(slot, fresh, scale2, q_ref, *refs):
    outs, pack_ref = refs[6 + fresh : 9 + fresh], refs[9 + fresh]
    eye = iota((128, 128), 0) == iota((128, 128), 1)
    pack_ref[...] = jnp.zeros(pack_ref.shape, f32)

    def store(n, h, out, lse):
        for k in range(3):
            at = slice(128 * k, 128 * k + 128)
            outs[k][0, 128 * h : 128 * h + 128, :] = out[at]
            for m, x in enumerate(split3(stat_row(eye, lse[at]))):
                pack_ref[k, 2 * m + h : 2 * m + h + 1, :] = x

    attention_core([[(q_ref, k, 4 * slot + k) for k in (1, 2, 3)]], refs[:6], store, scale2)
    for k in range(3):
        outs[k][0, 256:272, :] = pack_ref[k].astype(bf16)


def stay_kernel(scale2, *refs):
    out_ref, pack_ref = refs[14], refs[15]
    eye = iota((128, 128), 0) == iota((128, 128), 1)
    pack_ref[...] = jnp.zeros(pack_ref.shape, f32)

    def store(n, h, out, lse):
        for k in range(2):
            at = slice(128 * k, 128 * k + 128)
            out_ref[2 * n + k, 128 * h : 128 * h + 128, :] = out[at]
            for m, x in enumerate(split3(stat_row(eye, lse[at]))):
                pack_ref[2 * n + k, 2 * m + h : 2 * m + h + 1, :] = x

    items = [[(refs[2 * n + k], 0, 4 * (2 * n + k)) for k in range(2)] for n in range(4)]
    attention_core(items, refs[8:14], store, scale2)
    for slot in range(8):
        out_ref[slot, 256:272, :] = pack_ref[slot].astype(bf16)


scale2 = math.log2(math.e) / math.sqrt(128)


def attention_away(slot, q, fixed, prior):
    part, at = (first, slot) if slot < first else (8 - first, slot - first)
    shape = jax.ShapeDtypeStruct((part, 272, 128), bf16)
    return pl.pallas_call(
        functools.partial(away_kernel, slot, len(prior), scale2),
        grid=(1,),
        out_shape=(shape,) * 3,
        in_specs=[VMEM] * 7 + [ANY] * len(prior),
        out_specs=(pl.BlockSpec((1, 272, 128), lambda i: (at, 0, 0)),) * 3,
        scratch_shapes=[pltpu.VMEM((3, 16, 128), f32)],
        input_output_aliases={7 + i: i for i in range(len(prior))},
        compiler_params=pltpu.CompilerParams(vmem_limit_bytes=40 * MIB),
        cost_estimate=pl.CostEstimate(flops=2_300_000_000, bytes_accessed=4_000_000, transcendentals=0),
        name="attention_away",
    )(q, *fixed, *prior)


def attention_stay(blocks, fixed):
    return pl.pallas_call(
        functools.partial(stay_kernel, scale2),
        out_shape=jax.ShapeDtypeStruct((8, 272, 128), bf16),
        in_specs=[VMEM] * 14,
        out_specs=VMEM,
        scratch_shapes=[pltpu.VMEM((8, 16, 128), f32)],
        compiler_params=pltpu.CompilerParams(vmem_limit_bytes=40 * MIB),
        cost_estimate=pl.CostEstimate(flops=6_000_000_000, bytes_accessed=4_000_000, transcendentals=0),
        name="attention_stay",
    )(*blocks, *fixed)


def mix(eye, weights, blocks):
    acc = jnp.zeros((128, 128), f32)
    for w, b in zip(weights, blocks):
        d = jnp.where(eye, jnp.broadcast_to(w, (128, 128)), 0.0)
        hi = d.astype(bf16)
        lo = (d - hi.astype(f32)).astype(bf16)
        acc = acc + jnp.dot(hi, b, preferred_element_type=f32)
        acc = acc + jnp.dot(lo, b, preferred_element_type=f32)
    return acc.astype(bf16)


def slab_kernel(*refs):
    msgs, out_ref, st_ref, pack_ref = refs[:7], refs[7], refs[8], refs[9]
    z = lax.axis_index("z")
    eye = iota((128, 128), 0) == iota((128, 128), 1)
    row = iota((16, 128), 0)

    def sources(slot):
        if slot < first:
            return [(msgs[0], slot)] + [(m, slot) for m in msgs[1:4]]
        return [(msgs[0], slot)] + [(m, slot - first) for m in msgs[4:7]]

    for slot in range(8):
        for n, (m, s) in enumerate(sources(slot)):
            x = m[s, 256:272, :].astype(f32)
            for h in range(2):
                own = (row < 6) & (row % 2 == h)
                lse = jnp.sum(jnp.where(own, x, 0.0), axis=0, keepdims=True)
                st_ref[n, 2 * slot + h : 2 * slot + h + 1, :] = lse
    lses = [st_ref[n] for n in range(4)]
    top = functools.reduce(jnp.maximum, lses)
    weights = [jnp.exp2(x - top) for x in lses]
    total = functools.reduce(jnp.add, weights)
    weights = [x / total for x in weights]
    parts = split3(top + jnp.log2(total))
    pack_ref[...] = jnp.zeros((2, 16, 128), f32)
    for slot in range(8):
        at = ((z + 8 + offsets[slot]) % 8) * 2
        for h in range(2):
            i = 2 * slot + h
            blocks = [m[s, 128 * h : 128 * h + 128, :] for m, s in sources(slot)]
            mixed = mix(eye, [w[i : i + 1] for w in weights], blocks)
            for j in range(2):
                out_ref[at + j, 64 * h : 64 * h + 64, :] = mixed[64 * j : 64 * j + 64]
        i = 2 * slot
        for n, x in enumerate(parts):
            a, b = x[i : i + 1], x[i + 1 : i + 2]
            pack_ref[0, n : n + 1, :] = jnp.concatenate([a[:, :64], b[:, :64]], axis=1)
            pack_ref[1, n : n + 1, :] = jnp.concatenate([a[:, 64:], b[:, 64:]], axis=1)
        for j in range(2):
            out_ref[at + j, 128:144, :] = pack_ref[j].astype(bf16)


def slab_combine(msgs):
    return pl.pallas_call(
        slab_kernel,
        out_shape=jax.ShapeDtypeStruct((16, 144, 128), bf16),
        in_specs=[VMEM] * 7,
        out_specs=VMEM,
        scratch_shapes=[pltpu.VMEM((4, 16, 128), f32), pltpu.VMEM((2, 16, 128), f32)],
        compiler_params=pltpu.CompilerParams(vmem_limit_bytes=24 * MIB),
        cost_estimate=pl.CostEstimate(flops=500_000_000, bytes_accessed=3_000_000, transcendentals=0),
        name="slab_combine",
    )(*msgs)


def home_kernel(m_ref, out_ref, st_ref):
    eye = iota((128, 128), 0) == iota((128, 128), 1)
    for n in range(16):
        x = m_ref[n, 128:144, :].astype(f32)
        st_ref[n : n + 1, :] = jnp.sum(jnp.where(iota((16, 128), 0) < 3, x, 0.0), axis=0, keepdims=True)
    lse = st_ref[...]
    weights = jnp.exp2(lse - jnp.max(lse, axis=0, keepdims=True))
    weights = weights / jnp.sum(weights, axis=0, keepdims=True)
    mixed = mix(eye, [weights[n : n + 1] for n in range(16)], [m_ref[n, 0:128, :] for n in range(16)])
    for h in range(2):
        for t in range(4):
            at = 64 * h + 16 * t
            out_ref[t, 16 * h : 16 * h + 16, :] = mixed[at : at + 16]


def home_combine(msgs):
    return pl.pallas_call(
        home_kernel,
        out_shape=jax.ShapeDtypeStruct((4, 32, 128), bf16),
        in_specs=[VMEM],
        out_specs=VMEM,
        scratch_shapes=[pltpu.VMEM((16, 128), f32)],
        compiler_params=pltpu.CompilerParams(vmem_limit_bytes=8 * MIB),
        name="home_combine",
    )(msgs)


def project_kernel(n, *refs):
    x = jnp.concatenate([r[...] for r in refs[:n]], axis=0)
    for c in range(2):
        y = jnp.dot(x, refs[n + c][...], preferred_element_type=f32).astype(bf16)
        for i in range(n):
            refs[n + 2][c, i] = y[32 * i : 32 * i + 32]


def project(blocks, weights):
    n = len(blocks)
    return pl.pallas_call(
        functools.partial(project_kernel, n),
        out_shape=jax.ShapeDtypeStruct((2, n, 32, 256), bf16),
        in_specs=[VMEM] * (n + 2),
        out_specs=VMEM,
        compiler_params=pltpu.CompilerParams(vmem_limit_bytes=24 * MIB),
        cost_estimate=pl.CostEstimate(flops=1_000_000_000, bytes_accessed=5_000_000, transcendentals=0),
        name="project",
    )(*blocks, *weights)


def shift(x, axis, k, size):
    return lax.ppermute(x, axis, [(i, (i + k) % size) for i in range(size)])


def spread(x, axes, n):
    return lax.all_to_all(jnp.broadcast_to(x[None], (n,) + x.shape), axes, 0, 0)


def per_device(queries, cached_keys, cached_values, cached_pos, new_keys, new_values, new_pos, out_weight):
    z, y, xl = lax.axis_index("z"), lax.axis_index("y"), lax.axis_index("xl")

    block = spread(queries, ("y", "xl"), 8).reshape(32, 32, 128)
    fixed = prepare(new_pos, cached_pos, cached_keys, cached_values, new_keys, new_values)
    other_weight = shift(out_weight, "xl", 1, 2)

    msgs = attention_away(0, block, fixed, ())
    up, down = block, block
    blocks = [block]
    part = None
    for s in (1, 2, 3):
        up, down = shift(up, "z", 1, 8), shift(down, "z", -1, 8)
        blocks += [up, down]
        for slot in (2 * s - 1, 2 * s):
            msgs = attention_away(slot, blocks[slot], fixed, msgs)
            if slot == first - 1:
                part, msgs = msgs, ()
    blocks.append(shift(up, "z", 1, 8))
    msgs = attention_away(7, blocks[7], fixed, msgs)
    stay = attention_stay(blocks, fixed)

    away = [shift(m[k - 1], "y", k, 4) for m in (part, msgs) for k in (1, 2, 3)]
    pieces = slab_combine([stay] + away)
    pieces, other_weight = lax.optimization_barrier((pieces, other_weight))

    final = home_combine(lax.all_to_all(pieces, ("z", "xl"), 0, 0, tiled=True))
    context = final.reshape(4, 4096)
    slab = spread(context, ("z",), 8).reshape(32, 4096)

    ahead, behind, far = shift(slab, "y", -1, 4), shift(slab, "y", 1, 4), shift(slab, "y", 2, 4)
    weights = (out_weight, other_weight)
    near = project((slab, ahead, behind), weights)
    terms = [near[:, 0:1], near[:, 1:2], project((far,), weights), near[:, 2:3]]
    terms = [x.reshape(2, 1, 4, 2, 4, 256) for x in terms]
    terms = jnp.concatenate(terms + terms[:3], axis=1)
    terms = lax.dynamic_slice_in_dim(terms, (4 - y) % 4, 4, axis=1)
    terms = jnp.where(xl == 0, terms, terms[::-1])
    terms = jnp.transpose(terms, (0, 2, 3, 1, 4, 5)).reshape(8, 32, 256)
    parts = lax.all_to_all(terms, ("xl", "xh", "core"), 0, 0, tiled=True)
    projected = jnp.sum(parts.reshape(2, 4, 8, 4, 256).astype(f32), axis=1).astype(bf16)
    projected = jnp.transpose(projected, (1, 0, 2, 3)).reshape(64, 256)
    return (context, projected)


def solution(mesh):
    fine = Mesh(mesh.devices.reshape(8, 4, 2, 2, 2), ("z", "y", "xl", "xh", "core"))
    ctx, tp = ("z", "y", "xl"), ("xh", "core")
    in_specs = (
        P(ctx, tp, None),
        P(ctx, tp, None),
        P(ctx, tp, None),
        P(ctx),
        P(ctx, tp, None),
        P(ctx, tp, None),
        P(),
        P(tp, ctx),
    )
    out_specs = (P(ctx, tp), P(tp, ctx))
    return jax.shard_map(per_device, mesh=fine, in_specs=in_specs, out_specs=out_specs, check_vma=False)
```

```python
import functools
import math

import jax
import jax.numpy as jnp
from jax import lax
from jax.experimental import pallas as pl
from jax.experimental.pallas import tpu as pltpu
from jax.sharding import Mesh, PartitionSpec as P

bf16 = jnp.bfloat16
f32 = jnp.float32
masked_score = -1e30
VMEM = pl.BlockSpec(memory_space=pltpu.VMEM)
SMEM = pl.BlockSpec(memory_space=pltpu.SMEM)
ANY = pl.BlockSpec(memory_space=pl.ANY)
MIB = 1024 * 1024

offsets = (0, -1, 1, -2, 2, -3, 3, 4)
first = 5


def iota(shape, dim):
    return lax.broadcasted_iota(jnp.int32, shape, dim)


def split3(x):
    hi = x.astype(bf16).astype(f32)
    mid = (x - hi).astype(bf16).astype(f32)
    return hi, mid, x - hi - mid


def prepare_kernel(
    npos_ref, pos_ref, k_ref, v_ref, nk_ref, nv_ref, kt_ref, vx_ref, kn_ref, vn_ref, tok_ref, kpos_ref
):
    z, y, xl = lax.axis_index("z"), lax.axis_index("y"), lax.axis_index("xl")
    lane = iota((16, 128), 1)
    kpos = jnp.full((16, 128), 2**30, jnp.int32)
    for j in range(4):
        kpos = jnp.where(lane == j, npos_ref[((z * 4 + y) * 2 + xl) * 4 + j], kpos)
    kpos_ref[...] = kpos
    for slot in range(8):
        for k in range(4):
            at = ((z + 8 + offsets[slot]) % 8) * 32 + ((y + k) % 4) * 8
            for i in range(8):
                tok_ref[4 * slot + k, i : i + 1, :] = jnp.full((1, 128), npos_ref[at + i], jnp.int32)
    filled = jnp.sum((pos_ref[...] >= 0).astype(jnp.int32))
    step = 512
    slot0 = k_ref[0:16, :].astype(f32)[0:1]

    def body(i, carry):
        rows = pl.ds(pl.multiple_of(i * step, step), step)
        ok = iota((step, 128), 0) + i * step < filled
        for h in range(2):
            at = slice(128 * h, 128 * h + 128)
            k = k_ref[rows, at].astype(f32)
            kt_ref[h, rows, :] = jnp.where(ok, k, slot0[:, at]).astype(bf16)
            vx_ref[h, rows, 0:128] = jnp.where(ok, v_ref[rows, at].astype(f32), 0.0).astype(bf16)
            vx_ref[h, rows, 128:256] = jnp.where(ok, 1.0, 0.0).astype(bf16)
        return carry

    lax.fori_loop(0, 2048 // step, body, 0)
    nk, nv = nk_ref[...].astype(f32), nv_ref[...].astype(f32)
    for h in range(2):
        at = slice(128 * h, 128 * h + 128)
        pad = jnp.zeros((124, 128), f32)
        kn_ref[h] = jnp.concatenate([nk[:, at], pad], axis=0).astype(bf16)
        vn_ref[h, :, 0:128] = jnp.concatenate([nv[:, at], pad], axis=0).astype(bf16)
        vn_ref[h, :, 128:256] = jnp.ones((128, 128), bf16)


def prepare(new_pos, cached_pos, cached_keys, cached_values, new_keys, new_values):
    return pl.pallas_call(
        prepare_kernel,
        out_shape=(
            jax.ShapeDtypeStruct((2, 2048, 128), bf16),
            jax.ShapeDtypeStruct((2, 2048, 256), bf16),
            jax.ShapeDtypeStruct((2, 128, 128), bf16),
            jax.ShapeDtypeStruct((2, 128, 256), bf16),
            jax.ShapeDtypeStruct((32, 8, 128), jnp.int32),
            jax.ShapeDtypeStruct((16, 128), jnp.int32),
        ),
        in_specs=[SMEM] + [VMEM] * 5,
        out_specs=(VMEM,) * 6,
        compiler_params=pltpu.CompilerParams(vmem_limit_bytes=24 * MIB),
        cost_estimate=pl.CostEstimate(flops=500_000_000, bytes_accessed=6_000_000, transcendentals=0),
        name="prepare",
    )(
        new_pos,
        cached_pos.reshape(16, 128),
        cached_keys.reshape(2048, 256),
        cached_values.reshape(2048, 256),
        new_keys.reshape(4, 256),
        new_values.reshape(4, 256),
    )


def dot_t(a, b):
    return lax.dot_general(a, b, (((1,), (1,)), ((), ())), preferred_element_type=f32)


def attention_core(items, fixed_refs, store, scale2):
    kt_ref, vx_ref, kn_ref, vn_ref, tok_ref, kpos_ref = fixed_refs
    y = lax.axis_index("y")
    kpos = kpos_ref[...]

    def scores(chunk, h):
        heads = slice(16 * h, 16 * h + 16)
        q = [ref[pl.ds(((y + k) % 4) * 8, 8), heads, :] for ref, k, _ in chunk]
        q = jnp.concatenate(q, axis=0).reshape(128 * len(chunk), 128)
        s = dot_t(q, kt_ref[h])
        sn = dot_t(q, kn_ref[h])
        parts = []
        for n, (_, _, row) in enumerate(chunk):
            for i in range(8):
                at = 128 * n + 16 * i
                allow = kpos <= tok_ref[row, i : i + 1, :]
                parts.append(jnp.where(allow, sn[at : at + 16], masked_score))
        return s, jnp.concatenate(parts, axis=0)

    def finish(n, h, s, sn):
        top = jnp.maximum(jnp.max(s, axis=1, keepdims=True), jnp.max(sn, axis=1, keepdims=True))
        top = top * scale2
        p = jnp.exp2(s * scale2 - top).astype(bf16)
        pn = jnp.exp2(sn * scale2 - top).astype(bf16)
        acc = jnp.dot(p, vx_ref[h], preferred_element_type=f32)
        acc = acc + jnp.dot(pn, vn_ref[h], preferred_element_type=f32)
        total = acc[:, 128:]
        store(n, h, (acc[:, :128] / total).astype(bf16), top + jnp.log2(total))

    prev = None
    for n, chunk in enumerate(items):
        for h in range(2):
            s, sn = scores(chunk, h)
            if prev is not None:
                finish(*prev)
            prev = (n, h, s, sn)
    finish(*prev)


def stat_row(eye, lse):
    return jnp.sum(jnp.where(eye, lse, 0.0), axis=0, keepdims=True)


def away_kernel(slot, fresh, scale2, q_ref, *refs):
    outs, pack_ref = refs[6 + fresh : 9 + fresh], refs[9 + fresh]
    eye = iota((128, 128), 0) == iota((128, 128), 1)
    pack_ref[...] = jnp.zeros(pack_ref.shape, f32)

    def store(n, h, out, lse):
        for k in range(3):
            at = slice(128 * k, 128 * k + 128)
            outs[k][0, 128 * h : 128 * h + 128, :] = out[at]
            for m, x in enumerate(split3(stat_row(eye, lse[at]))):
                pack_ref[k, 2 * m + h : 2 * m + h + 1, :] = x

    attention_core([[(q_ref, k, 4 * slot + k) for k in (1, 2, 3)]], refs[:6], store, scale2)
    for k in range(3):
        outs[k][0, 256:272, :] = pack_ref[k].astype(bf16)


def stay_kernel(scale2, *refs):
    out_ref, pack_ref = refs[14], refs[15]
    eye = iota((128, 128), 0) == iota((128, 128), 1)
    pack_ref[...] = jnp.zeros(pack_ref.shape, f32)

    def store(n, h, out, lse):
        for k in range(2):
            at = slice(128 * k, 128 * k + 128)
            out_ref[2 * n + k, 128 * h : 128 * h + 128, :] = out[at]
            for m, x in enumerate(split3(stat_row(eye, lse[at]))):
                pack_ref[2 * n + k, 2 * m + h : 2 * m + h + 1, :] = x

    items = [[(refs[2 * n + k], 0, 4 * (2 * n + k)) for k in range(2)] for n in range(4)]
    attention_core(items, refs[8:14], store, scale2)
    for slot in range(8):
        out_ref[slot, 256:272, :] = pack_ref[slot].astype(bf16)


scale2 = math.log2(math.e) / math.sqrt(128)


def attention_away(slot, q, fixed, prior):
    part, at = (first, slot) if slot < first else (8 - first, slot - first)
    shape = jax.ShapeDtypeStruct((part, 272, 128), bf16)
    return pl.pallas_call(
        functools.partial(away_kernel, slot, len(prior), scale2),
        grid=(1,),
        out_shape=(shape,) * 3,
        in_specs=[VMEM] * 7 + [ANY] * len(prior),
        out_specs=(pl.BlockSpec((1, 272, 128), lambda i: (at, 0, 0)),) * 3,
        scratch_shapes=[pltpu.VMEM((3, 16, 128), f32)],
        input_output_aliases={7 + i: i for i in range(len(prior))},
        compiler_params=pltpu.CompilerParams(vmem_limit_bytes=40 * MIB),
        cost_estimate=pl.CostEstimate(flops=2_300_000_000, bytes_accessed=4_000_000, transcendentals=0),
        name="attention_away",
    )(q, *fixed, *prior)


def attention_stay(blocks, fixed):
    return pl.pallas_call(
        functools.partial(stay_kernel, scale2),
        out_shape=jax.ShapeDtypeStruct((8, 272, 128), bf16),
        in_specs=[VMEM] * 14,
        out_specs=VMEM,
        scratch_shapes=[pltpu.VMEM((8, 16, 128), f32)],
        compiler_params=pltpu.CompilerParams(vmem_limit_bytes=40 * MIB),
        cost_estimate=pl.CostEstimate(flops=6_000_000_000, bytes_accessed=4_000_000, transcendentals=0),
        name="attention_stay",
    )(*blocks, *fixed)


def mix(eye, weights, blocks):
    acc = jnp.zeros((128, 128), f32)
    for w, b in zip(weights, blocks):
        d = jnp.where(eye, jnp.broadcast_to(w, (128, 128)), 0.0)
        hi = d.astype(bf16)
        lo = (d - hi.astype(f32)).astype(bf16)
        acc = acc + jnp.dot(hi, b, preferred_element_type=f32)
        acc = acc + jnp.dot(lo, b, preferred_element_type=f32)
    return acc.astype(bf16)


def slab_kernel(*refs):
    msgs, out_ref, st_ref, pack_ref = refs[:7], refs[7], refs[8], refs[9]
    z = lax.axis_index("z")
    eye = iota((128, 128), 0) == iota((128, 128), 1)
    row = iota((16, 128), 0)

    def sources(slot):
        if slot < first:
            return [(msgs[0], slot)] + [(m, slot) for m in msgs[1:4]]
        return [(msgs[0], slot)] + [(m, slot - first) for m in msgs[4:7]]

    for slot in range(8):
        for n, (m, s) in enumerate(sources(slot)):
            x = m[s, 256:272, :].astype(f32)
            for h in range(2):
                own = (row < 6) & (row % 2 == h)
                lse = jnp.sum(jnp.where(own, x, 0.0), axis=0, keepdims=True)
                st_ref[n, 2 * slot + h : 2 * slot + h + 1, :] = lse
    lses = [st_ref[n] for n in range(4)]
    top = functools.reduce(jnp.maximum, lses)
    weights = [jnp.exp2(x - top) for x in lses]
    total = functools.reduce(jnp.add, weights)
    weights = [x / total for x in weights]
    parts = split3(top + jnp.log2(total))
    pack_ref[...] = jnp.zeros((2, 16, 128), f32)
    for slot in range(8):
        at = (z + 8 + offsets[slot]) % 8
        for h in range(2):
            i = 2 * slot + h
            blocks = [m[s, 128 * h : 128 * h + 128, :] for m, s in sources(slot)]
            mixed = mix(eye, [w[i : i + 1] for w in weights], blocks)
            for j in range(2):
                out_ref[at + 8 * j, 64 * h : 64 * h + 64, :] = mixed[64 * j : 64 * j + 64]
        i = 2 * slot
        for n, x in enumerate(parts):
            a, b = x[i : i + 1], x[i + 1 : i + 2]
            pack_ref[0, n : n + 1, :] = jnp.concatenate([a[:, :64], b[:, :64]], axis=1)
            pack_ref[1, n : n + 1, :] = jnp.concatenate([a[:, 64:], b[:, 64:]], axis=1)
        for j in range(2):
            out_ref[at + 8 * j, 128:144, :] = pack_ref[j].astype(bf16)


def slab_combine(msgs):
    return pl.pallas_call(
        slab_kernel,
        out_shape=jax.ShapeDtypeStruct((16, 144, 128), bf16),
        in_specs=[VMEM] * 7,
        out_specs=VMEM,
        scratch_shapes=[pltpu.VMEM((4, 16, 128), f32), pltpu.VMEM((2, 16, 128), f32)],
        compiler_params=pltpu.CompilerParams(vmem_limit_bytes=24 * MIB),
        cost_estimate=pl.CostEstimate(flops=500_000_000, bytes_accessed=3_000_000, transcendentals=0),
        name="slab_combine",
    )(*msgs)


def home_kernel(m_ref, out_ref, st_ref):
    eye = iota((128, 128), 0) == iota((128, 128), 1)
    for n in range(16):
        x = m_ref[n, 128:144, :].astype(f32)
        st_ref[n : n + 1, :] = jnp.sum(jnp.where(iota((16, 128), 0) < 3, x, 0.0), axis=0, keepdims=True)
    lse = st_ref[...]
    weights = jnp.exp2(lse - jnp.max(lse, axis=0, keepdims=True))
    weights = weights / jnp.sum(weights, axis=0, keepdims=True)
    mixed = mix(eye, [weights[n : n + 1] for n in range(16)], [m_ref[n, 0:128, :] for n in range(16)])
    for h in range(2):
        for t in range(4):
            at = 64 * h + 16 * t
            out_ref[t, 16 * h : 16 * h + 16, :] = mixed[at : at + 16]


def home_combine(msgs):
    return pl.pallas_call(
        home_kernel,
        out_shape=jax.ShapeDtypeStruct((4, 32, 128), bf16),
        in_specs=[VMEM],
        out_specs=VMEM,
        scratch_shapes=[pltpu.VMEM((16, 128), f32)],
        compiler_params=pltpu.CompilerParams(vmem_limit_bytes=8 * MIB),
        name="home_combine",
    )(msgs)


def project_kernel(n, *refs):
    x = jnp.concatenate([r[...] for r in refs[:n]], axis=0)
    for c in range(2):
        y = jnp.dot(x, refs[n + c][...], preferred_element_type=f32).astype(bf16)
        for i in range(n):
            refs[n + 2][c, i] = y[32 * i : 32 * i + 32]


def project(blocks, weights):
    n = len(blocks)
    return pl.pallas_call(
        functools.partial(project_kernel, n),
        out_shape=jax.ShapeDtypeStruct((2, n, 32, 256), bf16),
        in_specs=[VMEM] * (n + 2),
        out_specs=VMEM,
        compiler_params=pltpu.CompilerParams(vmem_limit_bytes=24 * MIB),
        cost_estimate=pl.CostEstimate(flops=1_000_000_000, bytes_accessed=5_000_000, transcendentals=0),
        name="project",
    )(*blocks, *weights)


def shift(x, axis, k, size):
    return lax.ppermute(x, axis, [(i, (i + k) % size) for i in range(size)])


def spread(x, axes, n):
    return lax.all_to_all(jnp.broadcast_to(x[None], (n,) + x.shape), axes, 0, 0)


def per_device(queries, cached_keys, cached_values, cached_pos, new_keys, new_values, new_pos, out_weight):
    z, y, xl = lax.axis_index("z"), lax.axis_index("y"), lax.axis_index("xl")

    other = shift(queries, "xl", 1, 2)
    pair = jnp.where(xl == 0, jnp.stack([queries, other]), jnp.stack([other, queries])).reshape(8, 32, 128)
    rows = [pair] + [shift(pair, "y", -k, 4) for k in (1, 2, 3)]
    block = lax.dynamic_slice_in_dim(jnp.concatenate(rows + rows[:3], axis=0), (4 - y) % 4 * 8, 32, axis=0)
    fixed = prepare(new_pos, cached_pos, cached_keys, cached_values, new_keys, new_values)
    other_weight = shift(out_weight, "xl", 1, 2)

    msgs = attention_away(0, block, fixed, ())
    up, down = block, block
    blocks = [block]
    part = None
    for s in (1, 2, 3):
        up, down = shift(up, "z", 1, 8), shift(down, "z", -1, 8)
        blocks += [up, down]
        for slot in (2 * s - 1, 2 * s):
            msgs = attention_away(slot, blocks[slot], fixed, msgs)
            if slot == first - 1:
                part, msgs = msgs, ()
    blocks.append(shift(up, "z", 1, 8))
    msgs = attention_away(7, blocks[7], fixed, msgs)
    stay = attention_stay(blocks, fixed)

    away = [shift(m[k - 1], "y", k, 4) for m in (part, msgs) for k in (1, 2, 3)]
    pieces = slab_combine([stay] + away)
    pieces, other_weight = lax.optimization_barrier((pieces, other_weight))

    final = home_combine(lax.all_to_all(pieces, ("xl", "z"), 0, 0, tiled=True))
    context = final.reshape(4, 4096)
    slab = spread(context, ("z",), 8).reshape(32, 4096)

    ahead, behind, far = shift(slab, "y", -1, 4), shift(slab, "y", 1, 4), shift(slab, "y", 2, 4)
    weights = (out_weight, other_weight)
    near = project((slab, ahead, behind), weights)
    terms = [near[:, 0:1], near[:, 1:2], project((far,), weights), near[:, 2:3]]
    terms = [x.reshape(2, 1, 4, 2, 4, 256) for x in terms]
    terms = jnp.concatenate(terms + terms[:3], axis=1)
    terms = lax.dynamic_slice_in_dim(terms, (4 - y) % 4, 4, axis=1)
    terms = jnp.where(xl == 0, terms, terms[::-1])
    terms = jnp.transpose(terms, (0, 2, 3, 1, 4, 5)).reshape(8, 32, 256)
    parts = lax.all_to_all(terms, ("xl", "xh", "core"), 0, 0, tiled=True)
    projected = jnp.sum(parts.reshape(2, 4, 8, 4, 256).astype(f32), axis=1).astype(bf16)
    projected = jnp.transpose(projected, (1, 0, 2, 3)).reshape(64, 256)
    return (context, projected)


def solution(mesh):
    fine = Mesh(mesh.devices.reshape(8, 4, 2, 2, 2), ("z", "y", "xl", "xh", "core"))
    ctx, tp = ("z", "y", "xl"), ("xh", "core")
    in_specs = (
        P(ctx, tp, None),
        P(ctx, tp, None),
        P(ctx, tp, None),
        P(ctx),
        P(ctx, tp, None),
        P(ctx, tp, None),
        P(),
        P(tp, ctx),
    )
    out_specs = (P(ctx, tp), P(tp, ctx))
    return jax.shard_map(per_device, mesh=fine, in_specs=in_specs, out_specs=out_specs, check_vma=False)
```
